256 devices in a mesh: tm: 16 (over x_hi, z), tile: 16 (over x_lo, y, core).
Axes of the slice: x: 4 (x_hi: 2, x_lo: 2; x = x_hi * 2 + x_lo), y: 4, z: 8, core: 2. Of those that a mesh axis runs over, the one named last changes fastest.
Arguments:
- initial: float32 [3, 512, 512], P(None, 'tile'), may hold values from -6 to 6
- rotation: float32 [512, 512], P('tile'), may hold values from -0.15 to 0.15
- seam_flip: int32 [16], replicated, may hold values from 0 to 1
Outputs:
- slice_ends: float32 [16, 3, 512, 512], P('tm', None, 'tile')
The draws below stay inside these ranges and needn't reach their ends.
All inputs are finite; a program needn't handle non-finite values.
Results may differ from the reference program's by a relative error of at most 0.0001.
Values sent between devices are 32-bit elements; how exact they have to be, the bound alone decides.
A program may use at most 64 MiB of HBM per device.

```python
import jax
import jax.numpy as jnp
from jax import lax

CY = 512
FSTEPS = 8
CSTEPS = 2
FACTOR = 4
SWEEPS = 2
TILES = 16
SLICES = 16
NX = 512


def place_ends(values, stream_key, least, high):
    shape = values.shape
    spot = [jax.random.randint(jax.random.fold_in(stream_key, axis), (), 0, shape[axis]) for axis in range(len(shape))]
    values = values.at[tuple(spot)].set(least)
    longest = shape.index(max(shape))
    spot[longest] = (spot[longest] + 1) % shape[longest]
    return values.at[tuple(spot)].set(high)


def block_scale(own_key, dims, split, least, largest):
    def one(axis_at, blocks):
        heights = jax.random.uniform(jax.random.fold_in(jax.random.fold_in(own_key, 6), axis_at), (blocks,), jnp.float32, least / len(split), largest / len(split))
        return jnp.repeat(jnp.exp(heights), dims[axis_at] // blocks).reshape((-1,) + (1,) * (len(dims) - axis_at - 1))

    level = one(*split[0])
    for cut in split[1:]:
        level = level * one(*cut)
    return level


def bell_draw(key, dims, scale, bound, cuts=(), dtype=jnp.bfloat16):
    gain = block_scale(key, dims, cuts, -0.22, 0.18) if cuts else 1.0
    entries = jax.random.normal(key, dims, jnp.float32) * scale * gain
    return jnp.minimum(jnp.maximum(entries, -bound), bound).astype(dtype)


def setup_inputs(seed: int = 0) -> dict:
    keys = jax.random.split(jax.random.key(seed), 4)
    return {
        "initial": bell_draw(keys[0], (3, NX, CY), 1.0, 6.0, ((1, 16),), jnp.float32),
        "rotation": jnp.clip(jax.random.uniform(keys[1], (NX, CY), jnp.float32, -0.15, 0.15) * block_scale(keys[1], (NX, CY), ((0, 16),), -0.4, 0.0), -0.15, 0.15),
        "seam_flip": place_ends(jax.random.randint(keys[2], (TILES,), 0, 2), jax.random.fold_in(keys[2], 1), 0, 1).astype(jnp.int32),
    }


courant = 0.9


def reflect(rim, flag, field_signs):
    return jnp.where(flag, field_signs * jnp.flip(rim, -1), rim)


def advance(extended, rotation_rate):
    height, flow_across, flow_along = extended[0], extended[1], extended[2]
    across_slope = (flow_across[..., 2:, :] - flow_across[..., :-2, :]) * 0.5
    along_mid = flow_along[..., 1:-1, :]
    along_slope = (jnp.roll(along_mid, -1, -1) - jnp.roll(along_mid, 1, -1)) * 0.5
    height_new = height[..., 1:-1, :] - courant * (across_slope + along_slope)
    height_core = height_new[..., 1:-1, :]
    height_across = (height_new[..., 2:, :] - height_new[..., :-2, :]) * 0.5
    height_along = (jnp.roll(height_core, -1, -1) - jnp.roll(height_core, 1, -1)) * 0.5
    across_core = flow_across[..., 2:-2, :]
    along_core = flow_along[..., 2:-2, :]
    across_new = across_core + rotation_rate * along_core - courant * height_across
    along_new = along_core - rotation_rate * across_new - courant * height_along
    return jnp.stack([height_core, across_new, along_new])


def restrict(field_in):
    field_shape = field_in.shape
    grouped = field_in.reshape(field_shape[:-2] + (field_shape[-2] // FACTOR, FACTOR, field_shape[-1] // FACTOR, FACTOR))
    return jnp.mean(grouped, axis=(-3, -1))


def prolong(field_in):
    return jnp.repeat(jnp.repeat(field_in, FACTOR, axis=-2), FACTOR, axis=-1)


def to_tiles(field_in):
    return field_in.reshape(field_in.shape[0], TILES, field_in.shape[1] // TILES, field_in.shape[2])


def untiled(blocks_in):
    return blocks_in.reshape(blocks_in.shape[0], -1, blocks_in.shape[3])


def extend(blocks_in, rim_width, lower_flip, upper_flip, field_signs):
    below = jnp.roll(blocks_in, 1, axis=1)[:, :, -rim_width:, :]
    above = jnp.roll(blocks_in, -1, axis=1)[:, :, :rim_width, :]
    return jnp.concatenate([reflect(below, lower_flip, field_signs), blocks_in, reflect(above, upper_flip, field_signs)], axis=2)


def reference(initial, rotation, seam_flip):
    lower_flip = (seam_flip != 0).reshape(1, TILES, 1, 1)
    upper_flip = (jnp.roll(seam_flip, -1) != 0).reshape(1, TILES, 1, 1)
    field_signs = jnp.array([1.0, 1.0, -1.0], jnp.float32).reshape(3, 1, 1, 1)
    rate_signs = jnp.array([-1.0], jnp.float32).reshape(1, 1, 1, 1)
    rim_coarse = 2 * CSTEPS
    fine_rate = to_tiles(rotation[None])[0]
    coarse_rate = extend(to_tiles((FACTOR * restrict(rotation))[None]), rim_coarse, lower_flip, upper_flip, rate_signs)[0]

    def fine_run(state):
        blocks_now = to_tiles(state)
        for substep in range(FSTEPS):
            blocks_now = advance(extend(blocks_now, 2, lower_flip, upper_flip, field_signs), fine_rate)
        return untiled(blocks_now)

    def coarse(state):
        extended = extend(to_tiles(state), rim_coarse, lower_flip, upper_flip, field_signs)
        for substep in range(CSTEPS):
            margin_rows = 2 + 2 * substep
            extended = advance(extended, coarse_rate[..., margin_rows:coarse_rate.shape[-2] - margin_rows, :])
        return untiled(extended)

    anchor = restrict(initial)
    first_old = coarse(anchor)
    old_terms = jnp.broadcast_to(first_old, (SLICES,) + first_old.shape)
    fine_all = jnp.broadcast_to(fine_run(initial), (SLICES,) + initial.shape)
    slice_ends = fine_all
    for sweep_index in range(SWEEPS):
        if sweep_index > 0:
            starts = jnp.concatenate([initial[None], slice_ends[:-1]], axis=0)
            fine_all = lax.map(fine_run, starts)
        coarse_fine = restrict(fine_all)
        offsets = coarse_fine - old_terms

        def chain_step(inbound, offset):
            advanced = coarse(inbound) + offset
            return advanced, advanced

        unused_state, chained = lax.scan(chain_step, anchor, offsets)
        old_terms = chained - offsets
        slice_ends = fine_all + prolong(chained - coarse_fine)
    return slice_ends
```

```python
import jax
import jax.numpy as jnp
from jax import lax
from jax.experimental import pallas as pl
from jax.experimental.pallas import tpu as pltpu
from jax.sharding import PartitionSpec as P

MESH = pl.DeviceIdType.MESH
NT = 16
NK = 16
HC = 0.45
FC = 24
FR = 88
CC = 80
CR = 168
ROUND_A = ((3, 2), (2, 1), (1, 1))
ROUND_B = ((12, 6), (8, 4), (4, 2))


def gather(x, idx):
    return jnp.take_along_axis(x, idx, axis=1)


def ahead(x):
    return pltpu.roll(x, 127, 1)


def behind(x):
    return pltpu.roll(x, 1, 1)


def coarse_step(st, e_ref, q, first, blocks):
    for b in range(blocks + 1):
        r = first - 1 + 8 * b
        g = st[0, pl.ds(r, 8), :] - HC * (st[1, pl.ds(r + 1, 8), :] - st[1, pl.ds(r - 1, 8), :])
        v = st[2, pl.ds(r, 8), :]
        wide = pltpu.roll(v, 126, 1) - 2.0 * v + pltpu.roll(v, 2, 1)
        st[0, pl.ds(r, 8), :] = g - HC * (ahead(v) - behind(v))
        e_ref[pl.ds(r, 8), :] = HC * ((ahead(g) - behind(g)) - HC * wide)
    for b in range(blocks):
        r = first + 8 * b
        u, v, rate = st[1, pl.ds(r, 8), :], st[2, pl.ds(r, 8), :], q[pl.ds(r, 8), :]
        new = u + rate * v - HC * (st[0, pl.ds(r + 1, 8), :] - st[0, pl.ds(r - 1, 8), :])
        st[1, pl.ds(r, 8), :] = new
        st[2, pl.ds(r, 8), :] = v - rate * new - e_ref[pl.ds(r, 8), :]


def coarse(st, e_ref, q, first, rows):
    coarse_step(st, e_ref, q, first - 2, rows // 8 + 1)
    coarse_step(st, e_ref, q, first, rows // 8)


def fine_step(st, e_ref, q, first, blocks):
    for b in range(blocks + 1):
        r = first - 1 + 8 * b
        v = [st[2, c, pl.ds(r, 8), :] for c in range(4)]
        g = [
            st[0, c, pl.ds(r, 8), :] - HC * (st[1, c, pl.ds(r + 1, 8), :] - st[1, c, pl.ds(r - 1, 8), :])
            for c in range(4)
        ]
        vs = [behind(v[2]), behind(v[3])] + v + [ahead(v[0]), ahead(v[1])]
        gs = [behind(g[3])] + g + [ahead(g[0])]
        for c in range(4):
            st[0, c, pl.ds(r, 8), :] = g[c] - HC * (vs[c + 3] - vs[c + 1])
            e_ref[c, pl.ds(r, 8), :] = HC * ((gs[c + 2] - gs[c]) - HC * (vs[c + 4] - 2.0 * v[c] + vs[c]))
    for b in range(blocks):
        r = first + 8 * b
        for c in range(4):
            u, v, rate = st[1, c, pl.ds(r, 8), :], st[2, c, pl.ds(r, 8), :], q[c, pl.ds(r, 8), :]
            new = u + rate * v - HC * (st[0, c, pl.ds(r + 1, 8), :] - st[0, c, pl.ds(r - 1, 8), :])
            st[1, c, pl.ds(r, 8), :] = new
            st[2, c, pl.ds(r, 8), :] = v - rate * new - e_ref[c, pl.ds(r, 8), :]


def fine_run(st, e_ref, q):
    for first, blocks in ((0, 8), (2, 7), (4, 6), (6, 5)):
        def one(s, carry, first=first, blocks=blocks):
            fine_step(st, e_ref, q, 10 + 2 * (first + s), blocks)
            return carry

        lax.fori_loop(0, 2, one, 0)


def restrict(ref, first):
    total = None
    for j in range(4):
        for c in range(4):
            part = ref[c, pl.ds(first + j, 8, stride=4), :]
            total = part if total is None else total + part
    return total


def kernel(initial, rotation, flips, out, xin, rin, own, own_q, halo, halo_q, fine, fine_q, fine_e, first_run, halo_f,
           rates, rate_own, rate_ring, start_own, start_ring, ring, ring_e, total, anchor_old, work, term_own, term_in,
           part_own, part_in, fine_out, load_sem, send_sem, halo_sem, ring_sem, a_sem, b_sem):
    k = lax.axis_index("tm")
    t = lax.axis_index("tile")
    lane = lax.broadcasted_iota(jnp.int32, (8, 128), 1)
    turned = 127 - lane

    def tile_at(o):
        return lax.rem(t + (o + NT), NT)

    load_x = pltpu.make_async_copy(initial, xin, load_sem.at[0])
    load_q = pltpu.make_async_copy(rotation, rin, load_sem.at[1])
    load_x.start()
    load_q.start()

    barrier = pltpu.get_barrier_semaphore()
    for o in range(1, NT):
        pl.semaphore_signal(barrier, inc=1, device_id=(k, tile_at(o)), device_id_type=MESH)
    expected = NT - 1
    for distance, reach in ROUND_A + ROUND_B:
        @pl.when(k >= distance)
        def _(distance=distance, reach=reach):
            for o in range(-reach, reach + 1):
                pl.semaphore_signal(barrier, inc=1, device_id=(k - distance, tile_at(o)), device_id_type=MESH)

        expected = expected + jnp.where(k + distance < NK, 2 * reach + 1, 0)

    odd = {0: None}
    up = down = jnp.int32(0)
    for o in range(1, NT // 2 + 1):
        up = up + jnp.where(flips[tile_at(o)] != 0, 1, 0)
        down = down + jnp.where(flips[tile_at(1 - o)] != 0, 1, 0)
        odd[o] = (jnp.zeros((8, 128), jnp.int32) + lax.rem(up, 2)) != 0
        odd[-o] = (jnp.zeros((8, 128), jnp.int32) + lax.rem(down, 2)) != 0

    def turn(x, o, negate, other=None):
        if o == 0:
            return x
        back = gather(x if other is None else other, turned)
        return jnp.where(odd[o], -back if negate else back, x)

    def oriented(src, o):
        return [turn(src[f], o, f == 2) for f in range(3)]

    zero = jnp.zeros((8, 128), jnp.float32)
    for f in range(3):
        for b in range(CR // 8):
            work[f, 8 * b : 8 * b + 8, :] = zero
        for b in (0, 1, CR // 8 - 2, CR // 8 - 1):
            ring[f, 8 * b : 8 * b + 8, :] = zero
        for c in range(4):
            for b in (0, FR // 8 - 2, FR // 8 - 1):
                fine[f, c, 8 * b : 8 * b + 8, :] = zero
        total[f] = jnp.zeros((16, 128), jnp.float32)
    for b in (0, 1, CR // 8 - 2, CR // 8 - 1):
        rates[8 * b : 8 * b + 8, :] = zero
    for c in range(4):
        for b in (0, FR // 8 - 2, FR // 8 - 1):
            fine_q[c, 8 * b : 8 * b + 8, :] = zero

    quarter = lane // 32
    apart = 4 * lax.rem(lane, 32)

    def spread(load, store):
        x = [load(s) for s in range(4)]
        for c in range(4):
            y = [gather(x[s], apart + c) for s in range(4)]
            store(c, jnp.where(quarter < 2, jnp.where(quarter == 0, y[0], y[1]), jnp.where(quarter == 2, y[2], y[3])))

    load_q.wait()
    for b in range(4):
        def store_q(c, x, b=b):
            own_q[c, 8 * b : 8 * b + 8, :] = x
            fine_q[c, FC + 8 * b : FC + 8 * b + 8, :] = x

        spread(lambda s, b=b: rin[8 * b : 8 * b + 8, 128 * s : 128 * s + 128], store_q)
    load_x.wait()
    for f in range(3):
        for b in range(4):
            def store_x(c, x, f=f, b=b):
                own[f, c, 8 * b : 8 * b + 8, :] = x
                fine[f, c, FC + 8 * b : FC + 8 * b + 8, :] = x

            spread(lambda s, f=f, b=b: xin[f, 8 * b : 8 * b + 8, 128 * s : 128 * s + 128], store_x)

    pl.semaphore_wait(barrier, expected)

    def send(src, dst, recv, where):
        pltpu.make_async_remote_copy(
            src_ref=src, dst_ref=dst, send_sem=send_sem, recv_sem=recv, device_id=where, device_id_type=MESH
        ).start()

    def take(ref, sem):
        pltpu.make_async_copy(ref, ref, sem).wait()

    send(own.at[:, :, pl.ds(16, 16), :], halo.at[0], halo_sem.at[0], (k, tile_at(1)))
    send(own.at[:, :, pl.ds(0, 16), :], halo.at[1], halo_sem.at[1], (k, tile_at(-1)))
    send(own_q.at[:, pl.ds(16, 16), :], halo_q.at[0], halo_sem.at[2], (k, tile_at(1)))
    send(own_q.at[:, pl.ds(0, 16), :], halo_q.at[1], halo_sem.at[3], (k, tile_at(-1)))
    rate_own[...] = restrict(own_q, 0) * 0.25
    for o in range(1, NT):
        send(rate_own, rate_ring.at[NT - o - 1], ring_sem.at[0], (k, tile_at(o)))

    take(halo_q.at[0], halo_sem.at[2])
    take(halo_q.at[1], halo_sem.at[3])
    for side, o, row in ((0, -1, FC - 16), (1, 1, FC + 32)):
        for b in range(2):
            for c in range(4):
                x, y = (halo_q[side, cc, 8 * b : 8 * b + 8, :] for cc in (c, 3 - c))
                fine_q[c, row + 8 * b : row + 8 * b + 8, :] = turn(x, o, True, y)

    def fill_rims(src, sem):
        for side, o, row in ((0, -1, FC - 16), (1, 1, FC + 32)):
            take(src.at[side], sem.at[side])
            for f in range(3):
                for b in range(2):
                    for c in range(4):
                        x, y = (src[side, f, cc, 8 * b : 8 * b + 8, :] for cc in (c, 3 - c))
                        fine[f, c, row + 8 * b : row + 8 * b + 8, :] = turn(x, o, f == 2, y)

    fill_rims(halo, halo_sem)
    for f in range(3):
        for half in range(2):
            work[f, pl.ds(CC - 4 + 8 * half, 8), :] = restrict(fine.at[f], FC - 16 + 32 * half) * 0.0625
        anchor_old[f] = work[f, pl.ds(CC, 8), :]
    fine_run(fine, fine_e, fine_q)
    for f in range(3):
        start = restrict(fine.at[f], FC) * 0.0625 - anchor_old[f]
        start_own[f] = start
        ring[f, CC : CC + 8, :] = start
    for o in range(1, NT):
        send(start_own, start_ring.at[NT - o - 1], ring_sem.at[1], (k, tile_at(o)))
    for f in range(3):
        for c in range(4):
            first_run[f, c] = fine[f, c, FC : FC + 32, :]
    send(first_run.at[:, :, pl.ds(16, 16), :], halo_f.at[0], halo_sem.at[4], (k, tile_at(1)))
    send(first_run.at[:, :, pl.ds(0, 16), :], halo_f.at[1], halo_sem.at[5], (k, tile_at(-1)))

    offsets = [o for o in range(-(NT // 2), NT // 2 + 1) if o]
    take(rate_ring, ring_sem.at[0])
    rates[CC : CC + 8, :] = rate_own[...]
    for o in offsets:
        rates[CC + 8 * o : CC + 8 * o + 8, :] = turn(rate_ring[(o + NT) % NT - 1], o, True)
    coarse(work, ring_e, rates, CC, 8)
    for f in range(3):
        anchor_old[f] = work[f, CC : CC + 8, :]

    take(start_ring, ring_sem.at[1])
    for o in offsets:
        for f, x in enumerate(oriented(start_ring.at[(o + NT) % NT - 1], o)):
            ring[f, CC + 8 * o : CC + 8 * o + 8, :] = x

    for m in (3, 2, 1, 0):
        def chain(s, carry, m=m):
            coarse(ring, ring_e, rates, CC - 16 - 16 * m, 40 + 32 * m)
            for f in range(3):
                total[f] = total[f] + ring[f, pl.ds(CC - 4, 16), :]
            return carry

        lax.fori_loop(0, jnp.clip(k - 1 - 4 * m, 0, 4), chain, 0)

    fill_rims(halo_f, halo_sem.at[pl.ds(4, 2)])
    for f in range(3):
        more = total[f]
        for c in range(4):
            for j in range(4):
                rows = pl.ds(FC - 16 + j, 16, stride=4)
                fine[f, c, rows, :] = fine[f, c, rows, :] + more
    coarse(ring, ring_e, rates, CC, 8)
    for f in range(3):
        anchor_old[f] = anchor_old[f] + total[f, pl.ds(4, 8), :] + ring[f, CC : CC + 8, :]
    fine_run(fine, fine_e, fine_q)

    @pl.when(k == 0)
    def _():
        for f in range(3):
            anchor_old[f] = zero
            for c in range(4):
                fine[f, c, FC : FC + 32, :] = first_run[f, c]

    for f in range(3):
        mean = restrict(fine.at[f], FC) * 0.0625
        start_own_f = mean - anchor_old[f]
        total[f, 0:8, :] = mean
        term_own[f] = start_own_f

    def places(stages):
        at, base = {}, 0
        for distance, reach in stages:
            at[distance] = base
            base += 2 * reach + 1
        return at

    def prefix(stages, src, landing, sems, applications):
        at = places(stages)
        for stage, (distance, reach) in reversed(list(enumerate(stages))):
            @pl.when(k + distance < NK)
            def _(stage=stage, distance=distance, reach=reach):
                for o in range(-reach, reach + 1):
                    send(src, landing.at[at[distance] + reach - o], sems.at[stage], (k + distance, tile_at(o)))

        for stage, (distance, reach) in enumerate(stages):
            @pl.when(k >= distance)
            def _(stage=stage, distance=distance, reach=reach):
                base = at[distance]
                take(landing.at[pl.ds(base, 2 * reach + 1)], sems.at[stage])
                for o in range(-reach, reach + 1):
                    for f, x in enumerate(oriented(landing.at[base + reach + o], o)):
                        rows = slice(CC + 8 * o, CC + 8 * o + 8)
                        work[f, rows, :] = work[f, rows, :] + x
                if applications == 1:
                    coarse(work, ring_e, rates, CC - 4 * (distance - 1), 8 * distance)
                else:
                    def apply(s, carry):
                        coarse(work, ring_e, rates, CC - 4 * (distance - 1), 8 * distance)
                        return carry

                    lax.fori_loop(0, applications, apply, 0)

    def clear():
        for f in range(3):
            for b in range(CR // 8):
                work[f, 8 * b : 8 * b + 8, :] = zero

    clear()
    prefix(ROUND_A, term_own, term_in, a_sem, 1)
    for f in range(3):
        part_own[f] = work[f, CC : CC + 8, :] + term_own[f]
    clear()
    prefix(ROUND_B, part_own, part_in, b_sem, 4)

    apart_out = lane // 4
    phase = lax.rem(lane, 4)
    for f in range(3):
        extra = work[f, CC : CC + 8, :] + part_own[f] - total[f, 0:8, :]
        for c in range(4):
            for j in range(4):
                rows = pl.ds(FC + j, 8, stride=4)
                fine[f, c, rows, :] = fine[f, c, rows, :] + extra
        for b in range(4):
            z = [fine[f, c, FC + 8 * b : FC + 8 * b + 8, :] for c in range(4)]
            for s in range(4):
                y = [gather(z[c], apart_out + 32 * s) for c in range(4)]
                out[0, f, 8 * b : 8 * b + 8, 128 * s : 128 * s + 128] = jnp.where(
                    phase < 2, jnp.where(phase == 0, y[0], y[1]), jnp.where(phase == 2, y[2], y[3])
                )

    for _ in range(2):
        take(halo, send_sem)
    take(halo_q, send_sem)
    take(rate_ring, send_sem)
    take(start_ring, send_sem)
    for stages, landing in ((ROUND_A, term_in), (ROUND_B, part_in)):
        at = places(stages)
        for distance, reach in stages:
            @pl.when(k + distance < NK)
            def _(landing=landing, base=at[distance], count=2 * reach + 1):
                take(landing.at[pl.ds(base, count)], send_sem)


def body(initial, rotation, seam_flip):
    def vmem(*shape):
        return pltpu.VMEM(shape, jnp.float32)

    dma = pltpu.SemaphoreType.DMA
    scratch = [
        vmem(3, 32, 512), vmem(32, 512),
        vmem(3, 4, 32, 128), vmem(4, 32, 128),
        vmem(2, 3, 4, 16, 128), vmem(2, 4, 16, 128),
        vmem(3, 4, FR, 128), vmem(4, FR, 128), vmem(4, FR, 128),
        vmem(3, 4, 32, 128), vmem(2, 3, 4, 16, 128),
        vmem(CR, 128), vmem(8, 128), vmem(NT - 1, 8, 128),
        vmem(3, 8, 128), vmem(NT - 1, 3, 8, 128),
        vmem(3, CR, 128), vmem(CR, 128),
        vmem(3, 16, 128), vmem(3, 8, 128),
        vmem(3, CR, 128),
        vmem(3, 8, 128), vmem(11, 3, 8, 128),
        vmem(3, 8, 128), vmem(27, 3, 8, 128),
        vmem(8, 128),
        dma((2,)), dma, dma((6,)), dma((2,)), dma((3,)), dma((3,)),
    ]
    return pl.pallas_call(
        kernel,
        out_shape=jax.ShapeDtypeStruct((1, 3, 32, 512), jnp.float32),
        in_specs=[
            pl.BlockSpec(memory_space=pl.ANY),
            pl.BlockSpec(memory_space=pl.ANY),
            pl.BlockSpec(memory_space=pltpu.SMEM),
        ],
        out_specs=pl.BlockSpec(memory_space=pltpu.VMEM),
        scratch_shapes=scratch,
        compiler_params=pltpu.CompilerParams(
            collective_id=0, has_side_effects=True, vmem_limit_bytes=24 * 1024 * 1024
        ),
        name="parareal",
    )(initial, rotation, seam_flip)


def solution(mesh):
    in_specs = (P(None, "tile", None), P("tile", None), P())
    out_specs = P("tm", None, "tile", None)
    return jax.shard_map(body, mesh=mesh, in_specs=in_specs, out_specs=out_specs, check_vma=False)
```

```python
import jax
import jax.numpy as jnp
from jax import lax
from jax.experimental import pallas as pl
from jax.experimental.pallas import tpu as pltpu
from jax.sharding import PartitionSpec as P

MESH = pl.DeviceIdType.MESH
NT = 16
NK = 16
HC = 0.45
FC = 24
FR = 88
CC = 80
CR = 168
FAR_FIRST = tuple(range(NT // 2, 0, -1)) + tuple(range(-NT // 2 + 1, 0))
NZ = 8


def gather(x, idx):
    return jnp.take_along_axis(x, idx, axis=1)


def ahead(x):
    return pltpu.roll(x, 127, 1)


def behind(x):
    return pltpu.roll(x, 1, 1)


def coarse_step(st, e_ref, q, first, blocks):
    for b in range(blocks + 1):
        r = first - 1 + 8 * b
        g = st[0, pl.ds(r, 8), :] - HC * (st[1, pl.ds(r + 1, 8), :] - st[1, pl.ds(r - 1, 8), :])
        v = st[2, pl.ds(r, 8), :]
        wide = pltpu.roll(v, 126, 1) - 2.0 * v + pltpu.roll(v, 2, 1)
        st[0, pl.ds(r, 8), :] = g - HC * (ahead(v) - behind(v))
        e_ref[pl.ds(r, 8), :] = HC * ((ahead(g) - behind(g)) - HC * wide)
    for b in range(blocks):
        r = first + 8 * b
        u, v, rate = st[1, pl.ds(r, 8), :], st[2, pl.ds(r, 8), :], q[pl.ds(r, 8), :]
        new = u + rate * v - HC * (st[0, pl.ds(r + 1, 8), :] - st[0, pl.ds(r - 1, 8), :])
        st[1, pl.ds(r, 8), :] = new
        st[2, pl.ds(r, 8), :] = v - rate * new - e_ref[pl.ds(r, 8), :]


def coarse(st, e_ref, q, first, rows):
    coarse_step(st, e_ref, q, first - 2, rows // 8 + 1)
    coarse_step(st, e_ref, q, first, rows // 8)


def fine_step(st, e_ref, q, first, blocks):
    for b in range(blocks + 1):
        r = first - 1 + 8 * b
        v = [st[2, c, pl.ds(r, 8), :] for c in range(4)]
        g = [
            st[0, c, pl.ds(r, 8), :] - HC * (st[1, c, pl.ds(r + 1, 8), :] - st[1, c, pl.ds(r - 1, 8), :])
            for c in range(4)
        ]
        vs = [behind(v[2]), behind(v[3])] + v + [ahead(v[0]), ahead(v[1])]
        gs = [behind(g[3])] + g + [ahead(g[0])]
        for c in range(4):
            st[0, c, pl.ds(r, 8), :] = g[c] - HC * (vs[c + 3] - vs[c + 1])
            e_ref[c, pl.ds(r, 8), :] = HC * ((gs[c + 2] - gs[c]) - HC * (vs[c + 4] - 2.0 * v[c] + vs[c]))
    for b in range(blocks):
        r = first + 8 * b
        for c in range(4):
            u, v, rate = st[1, c, pl.ds(r, 8), :], st[2, c, pl.ds(r, 8), :], q[c, pl.ds(r, 8), :]
            new = u + rate * v - HC * (st[0, c, pl.ds(r + 1, 8), :] - st[0, c, pl.ds(r - 1, 8), :])
            st[1, c, pl.ds(r, 8), :] = new
            st[2, c, pl.ds(r, 8), :] = v - rate * new - e_ref[c, pl.ds(r, 8), :]


def fine_run(st, e_ref, q):
    for first, blocks in ((0, 8), (2, 7), (4, 6), (6, 5)):
        def one(s, carry, first=first, blocks=blocks):
            fine_step(st, e_ref, q, 10 + 2 * (first + s), blocks)
            return carry

        lax.fori_loop(0, 2, one, 0)


def restrict(ref, first):
    total = None
    for j in range(4):
        for c in range(4):
            part = ref[c, pl.ds(first + j, 8, stride=4), :]
            total = part if total is None else total + part
    return total


def kernel(initial, rotation, flips, out, xin, rin, own, own_q, halo, halo_q, fine, fine_q, fine_e, first_run, halo_f,
           rates, rate_own, rate_ring, start_own, start_ring, ring, ring_e, total, anchor_old, work, term_own, term_ring,
           powers, power_in, fine_out, load_sem, send_sem, halo_sem, ring_sem, power_sem, near_sem):
    k = lax.axis_index("tm")
    t = lax.axis_index("tile")
    lane = lax.broadcasted_iota(jnp.int32, (8, 128), 1)
    turned = 127 - lane

    def tile_at(o):
        return lax.rem(t + (o + NT), NT)

    load_x = pltpu.make_async_copy(initial, xin, load_sem.at[0])
    load_q = pltpu.make_async_copy(rotation, rin, load_sem.at[1])
    load_x.start()
    load_q.start()

    barrier = pltpu.get_barrier_semaphore()
    for o in range(1, NT):
        pl.semaphore_signal(barrier, inc=1, device_id=(k, tile_at(o)), device_id_type=MESH)
    slab, z = k // NZ, lax.rem(k, NZ)

    def slice_at(o):
        return slab * NZ + lax.rem(z + (o + NZ), NZ)

    across = lax.rem(slab + 1, 2) * NZ + z

    def meet(sem, slices):
        for other in slices:
            pl.semaphore_signal(sem, inc=1, device_id=(other, t), device_id_type=MESH)

    meet(barrier, (slice_at(1), slice_at(-1), across))
    odd = {0: None}
    up = down = jnp.int32(0)
    for o in range(1, NT // 2 + 1):
        up = up + jnp.where(flips[tile_at(o)] != 0, 1, 0)
        down = down + jnp.where(flips[tile_at(1 - o)] != 0, 1, 0)
        odd[o] = (jnp.zeros((8, 128), jnp.int32) + lax.rem(up, 2)) != 0
        odd[-o] = (jnp.zeros((8, 128), jnp.int32) + lax.rem(down, 2)) != 0

    def turn(x, o, negate, other=None):
        if o == 0:
            return x
        back = gather(x if other is None else other, turned)
        return jnp.where(odd[o], -back if negate else back, x)

    def oriented(src, o):
        return [turn(src[f], o, f == 2) for f in range(3)]

    zero = jnp.zeros((8, 128), jnp.float32)
    for f in range(3):
        for b in range(CR // 8):
            work[f, 8 * b : 8 * b + 8, :] = zero
        for b in (0, 1, CR // 8 - 2, CR // 8 - 1):
            ring[f, 8 * b : 8 * b + 8, :] = zero
        for c in range(4):
            for b in (0, FR // 8 - 2, FR // 8 - 1):
                fine[f, c, 8 * b : 8 * b + 8, :] = zero
        total[f] = jnp.zeros((16, 128), jnp.float32)
    for b in (0, 1, CR // 8 - 2, CR // 8 - 1):
        rates[8 * b : 8 * b + 8, :] = zero
    for c in range(4):
        for b in (0, FR // 8 - 2, FR // 8 - 1):
            fine_q[c, 8 * b : 8 * b + 8, :] = zero

    quarter = lane // 32
    apart = 4 * lax.rem(lane, 32)

    def spread(load, store):
        x = [load(s) for s in range(4)]
        for c in range(4):
            y = [gather(x[s], apart + c) for s in range(4)]
            store(c, jnp.where(quarter < 2, jnp.where(quarter == 0, y[0], y[1]), jnp.where(quarter == 2, y[2], y[3])))

    load_q.wait()
    for b in range(4):
        def store_q(c, x, b=b):
            own_q[c, 8 * b : 8 * b + 8, :] = x
            fine_q[c, FC + 8 * b : FC + 8 * b + 8, :] = x

        spread(lambda s, b=b: rin[8 * b : 8 * b + 8, 128 * s : 128 * s + 128], store_q)
    load_x.wait()
    for f in range(3):
        for b in range(4):
            def store_x(c, x, f=f, b=b):
                own[f, c, 8 * b : 8 * b + 8, :] = x
                fine[f, c, FC + 8 * b : FC + 8 * b + 8, :] = x

            spread(lambda s, f=f, b=b: xin[f, 8 * b : 8 * b + 8, 128 * s : 128 * s + 128], store_x)

    pl.semaphore_wait(barrier, NT + 2)
    meet(near_sem.at[0], (slice_at(1), slice_at(-1)))

    def send(src, dst, recv, where, group=0):
        pltpu.make_async_remote_copy(
            src_ref=src, dst_ref=dst, send_sem=send_sem.at[group], recv_sem=recv, device_id=where, device_id_type=MESH
        ).start()

    def take(ref, sem):
        pltpu.make_async_copy(ref, ref, sem).wait()

    send(own.at[:, :, pl.ds(16, 16), :], halo.at[0], halo_sem.at[0], (k, tile_at(1)))
    send(own.at[:, :, pl.ds(0, 16), :], halo.at[1], halo_sem.at[1], (k, tile_at(-1)))
    send(own_q.at[:, pl.ds(16, 16), :], halo_q.at[0], halo_sem.at[2], (k, tile_at(1)))
    send(own_q.at[:, pl.ds(0, 16), :], halo_q.at[1], halo_sem.at[3], (k, tile_at(-1)))
    rate_own[...] = restrict(own_q, 0) * 0.25
    for o in FAR_FIRST:
        send(rate_own, rate_ring.at[(NT - o) % NT - 1], ring_sem.at[0], (k, tile_at(o)))

    take(halo_q.at[0], halo_sem.at[2])
    take(halo_q.at[1], halo_sem.at[3])
    for side, o, row in ((0, -1, FC - 16), (1, 1, FC + 32)):
        for b in range(2):
            for c in range(4):
                x, y = (halo_q[side, cc, 8 * b : 8 * b + 8, :] for cc in (c, 3 - c))
                fine_q[c, row + 8 * b : row + 8 * b + 8, :] = turn(x, o, True, y)

    def fill_rims(src, sem):
        for side, o, row in ((0, -1, FC - 16), (1, 1, FC + 32)):
            take(src.at[side], sem.at[side])
            for f in range(3):
                for b in range(2):
                    for c in range(4):
                        x, y = (src[side, f, cc, 8 * b : 8 * b + 8, :] for cc in (c, 3 - c))
                        fine[f, c, row + 8 * b : row + 8 * b + 8, :] = turn(x, o, f == 2, y)

    fill_rims(halo, halo_sem)
    pl.semaphore_wait(near_sem.at[0], 2)
    meet(near_sem.at[1], (slice_at(2), slice_at(-2)))
    for f in range(3):
        for half in range(2):
            work[f, pl.ds(CC - 4 + 8 * half, 8), :] = restrict(fine.at[f], FC - 16 + 32 * half) * 0.0625
        anchor_old[f] = work[f, pl.ds(CC, 8), :]
    fine_run(fine, fine_e, fine_q)
    for f in range(3):
        start = restrict(fine.at[f], FC) * 0.0625 - anchor_old[f]
        start_own[f] = start
        ring[f, CC : CC + 8, :] = start
    for o in FAR_FIRST:
        send(start_own, start_ring.at[(NT - o) % NT - 1], ring_sem.at[1], (k, tile_at(o)))
    for f in range(3):
        for c in range(4):
            first_run[f, c] = fine[f, c, FC : FC + 32, :]
    send(first_run.at[:, :, pl.ds(16, 16), :], halo_f.at[0], halo_sem.at[4], (k, tile_at(1)))
    send(first_run.at[:, :, pl.ds(0, 16), :], halo_f.at[1], halo_sem.at[5], (k, tile_at(-1)))

    offsets = [o for o in range(-(NT // 2), NT // 2 + 1) if o]
    take(rate_ring, ring_sem.at[0])
    rates[CC : CC + 8, :] = rate_own[...]
    for o in offsets:
        rates[CC + 8 * o : CC + 8 * o + 8, :] = turn(rate_ring[(o + NT) % NT - 1], o, True)
    coarse(work, ring_e, rates, CC, 8)
    for f in range(3):
        anchor_old[f] = work[f, CC : CC + 8, :]

    take(start_ring, ring_sem.at[1])
    for o in offsets:
        for f, x in enumerate(oriented(start_ring.at[(o + NT) % NT - 1], o)):
            ring[f, CC + 8 * o : CC + 8 * o + 8, :] = x

    pl.semaphore_wait(near_sem.at[1], 2)
    meet(near_sem.at[2], (across,))
    for m in (3, 2, 1, 0):
        def chain(s, carry, m=m):
            coarse(ring, ring_e, rates, CC - 16 - 16 * m, 40 + 32 * m)
            for f in range(3):
                total[f] = total[f] + ring[f, pl.ds(CC - 4, 16), :]
            return carry

        lax.fori_loop(0, jnp.clip(k - 1 - 4 * m, 0, 4), chain, 0)

    fill_rims(halo_f, halo_sem.at[pl.ds(4, 2)])

    for f in range(3):
        more = total[f]
        for c in range(4):
            for j in range(4):
                rows = pl.ds(FC - 16 + j, 16, stride=4)
                fine[f, c, rows, :] = fine[f, c, rows, :] + more
    coarse(ring, ring_e, rates, CC, 8)
    for f in range(3):
        anchor_old[f] = anchor_old[f] + total[f, pl.ds(4, 8), :] + ring[f, CC : CC + 8, :]
    fine_run(fine, fine_e, fine_q)

    @pl.when(k == 0)
    def _():
        for f in range(3):
            anchor_old[f] = zero
            for c in range(4):
                fine[f, c, FC : FC + 32, :] = first_run[f, c]

    for f in range(3):
        mean = restrict(fine.at[f], FC) * 0.0625
        start_own_f = mean - anchor_old[f]
        total[f, 0:8, :] = mean
        term_own[f] = start_own_f

    for o in FAR_FIRST:
        send(term_own, term_ring.at[(NT - o) % NT - 1], ring_sem.at[2], (k, tile_at(o)), 1)

    apart_out = lane // 4
    phase = lax.rem(lane, 4)
    for f in range(3):
        for b in range(4):
            x = [fine[f, c, FC + 8 * b : FC + 8 * b + 8, :] for c in range(4)]
            for s in range(4):
                y = [gather(x[c], apart_out + 32 * s) for c in range(4)]
                fine_out[f, s, 8 * b : 8 * b + 8, :] = jnp.where(
                    phase < 2, jnp.where(phase == 0, y[0], y[1]), jnp.where(phase == 2, y[2], y[3])
                )

    for f in range(3):
        work[f, CC : CC + 8, :] = term_own[f]
    take(term_ring, ring_sem.at[2])
    for o in offsets:
        for f, x in enumerate(oriented(term_ring.at[(o + NT) % NT - 1], o)):
            work[f, CC + 8 * o : CC + 8 * o + 8, :] = x
    pl.semaphore_wait(near_sem.at[2], 1)

    last = NK - 1 - k
    m = jnp.int32(0)
    for group in (3, 2, 1, 0):
        def power(s, m, group=group):
            coarse(work, ring_e, rates, CC - 12 - 16 * group, 32 + 32 * group)
            powers[m] = work[:, CC : CC + 8, :]
            send(powers.at[m], power_in.at[m], power_sem.at[m], (k + m + 1, t), 2)
            return m + 1

        m = lax.fori_loop(0, jnp.clip(last - 4 * group, 0, 4), power, m)

    def add(m, carry):
        take(power_in.at[m], power_sem.at[m])
        term_own[...] = term_own[...] + power_in[m]
        return carry

    take(term_ring, send_sem.at[1])
    lax.fori_loop(0, k, add, 0)

    for f in range(3):
        extra = term_own[f] - total[f, 0:8, :]
        for s in range(4):
            more = gather(extra, apart_out + 32 * s)
            for j in range(4):
                rows = pl.ds(j, 8, stride=4)
                fine_out[f, s, rows, :] = fine_out[f, s, rows, :] + more
            out[0, f, :, 128 * s : 128 * s + 128] = fine_out[f, s]

    for _ in range(2):
        take(halo, send_sem.at[0])
    take(halo_q, send_sem.at[0])
    take(rate_ring, send_sem.at[0])
    take(start_ring, send_sem.at[0])

    def sent(m, carry):
        take(powers.at[m], send_sem.at[2])
        return carry

    lax.fori_loop(0, last, sent, 0)


def body(initial, rotation, seam_flip):
    def vmem(*shape):
        return pltpu.VMEM(shape, jnp.float32)

    dma = pltpu.SemaphoreType.DMA
    scratch = [
        vmem(3, 32, 512), vmem(32, 512),
        vmem(3, 4, 32, 128), vmem(4, 32, 128),
        vmem(2, 3, 4, 16, 128), vmem(2, 4, 16, 128),
        vmem(3, 4, FR, 128), vmem(4, FR, 128), vmem(4, FR, 128),
        vmem(3, 4, 32, 128), vmem(2, 3, 4, 16, 128),
        vmem(CR, 128), vmem(8, 128), vmem(NT - 1, 8, 128),
        vmem(3, 8, 128), vmem(NT - 1, 3, 8, 128),
        vmem(3, CR, 128), vmem(CR, 128),
        vmem(3, 16, 128), vmem(3, 8, 128),
        vmem(3, CR, 128),
        vmem(3, 8, 128), vmem(NT - 1, 3, 8, 128),
        vmem(NK - 1, 3, 8, 128), vmem(NK - 1, 3, 8, 128),
        vmem(3, 4, 32, 128),
        dma((2,)), dma((3,)), dma((6,)), dma((3,)), dma((NK - 1,)), pltpu.SemaphoreType.REGULAR((3,)),
    ]
    return pl.pallas_call(
        kernel,
        out_shape=jax.ShapeDtypeStruct((1, 3, 32, 512), jnp.float32),
        in_specs=[
            pl.BlockSpec(memory_space=pl.ANY),
            pl.BlockSpec(memory_space=pl.ANY),
            pl.BlockSpec(memory_space=pltpu.SMEM),
        ],
        out_specs=pl.BlockSpec(memory_space=pltpu.VMEM),
        scratch_shapes=scratch,
        compiler_params=pltpu.CompilerParams(
            collective_id=0, has_side_effects=True, vmem_limit_bytes=60 * 1024 * 1024
        ),
        name="parareal",
    )(initial, rotation, seam_flip)


def solution(mesh):
    in_specs = (P(None, "tile", None), P("tile", None), P())
    out_specs = P("tm", None, "tile", None)
    return jax.shard_map(body, mesh=mesh, in_specs=in_specs, out_specs=out_specs, check_vma=False)
```

```python
import jax
import jax.numpy as jnp
from jax import lax
from jax.experimental import pallas as pl
from jax.experimental.pallas import tpu as pltpu
from jax.sharding import PartitionSpec as P

MESH = pl.DeviceIdType.MESH
NT = 16
NK = 16
HC = 0.45
FC = 24
FR = 88
CC = 80
CR = 168
NZ = 8
OTHERS = tuple((x, y, c) for y in (2, 1, 3, 0) for x in (1, 0) for c in (1, 0) if (x, y, c) != (0, 0, 0))


def gather(x, idx):
    return jnp.take_along_axis(x, idx, axis=1)


def ahead(x):
    return pltpu.roll(x, 127, 1)


def behind(x):
    return pltpu.roll(x, 1, 1)


def coarse_step(st, e_ref, q, first, blocks):
    for b in range(blocks + 1):
        r = first - 1 + 8 * b
        g = st[0, pl.ds(r, 8), :] - HC * (st[1, pl.ds(r + 1, 8), :] - st[1, pl.ds(r - 1, 8), :])
        v = st[2, pl.ds(r, 8), :]
        wide = pltpu.roll(v, 126, 1) - 2.0 * v + pltpu.roll(v, 2, 1)
        st[0, pl.ds(r, 8), :] = g - HC * (ahead(v) - behind(v))
        e_ref[pl.ds(r, 8), :] = HC * ((ahead(g) - behind(g)) - HC * wide)
    for b in range(blocks):
        r = first + 8 * b
        u, v, rate = st[1, pl.ds(r, 8), :], st[2, pl.ds(r, 8), :], q[pl.ds(r, 8), :]
        new = u + rate * v - HC * (st[0, pl.ds(r + 1, 8), :] - st[0, pl.ds(r - 1, 8), :])
        st[1, pl.ds(r, 8), :] = new
        st[2, pl.ds(r, 8), :] = v - rate * new - e_ref[pl.ds(r, 8), :]


def coarse(st, e_ref, q, first, rows):
    coarse_step(st, e_ref, q, first - 2, rows // 8 + 1)
    coarse_step(st, e_ref, q, first, rows // 8)


def fine_step(st, e_ref, q, first, blocks):
    for b in range(blocks + 1):
        r = first - 1 + 8 * b
        v = [st[2, c, pl.ds(r, 8), :] for c in range(4)]
        g = [
            st[0, c, pl.ds(r, 8), :] - HC * (st[1, c, pl.ds(r + 1, 8), :] - st[1, c, pl.ds(r - 1, 8), :])
            for c in range(4)
        ]
        vs = [behind(v[2]), behind(v[3])] + v + [ahead(v[0]), ahead(v[1])]
        gs = [behind(g[3])] + g + [ahead(g[0])]
        for c in range(4):
            st[0, c, pl.ds(r, 8), :] = g[c] - HC * (vs[c + 3] - vs[c + 1])
            e_ref[c, pl.ds(r, 8), :] = HC * ((gs[c + 2] - gs[c]) - HC * (vs[c + 4] - 2.0 * v[c] + vs[c]))
    for b in range(blocks):
        r = first + 8 * b
        for c in range(4):
            u, v, rate = st[1, c, pl.ds(r, 8), :], st[2, c, pl.ds(r, 8), :], q[c, pl.ds(r, 8), :]
            new = u + rate * v - HC * (st[0, c, pl.ds(r + 1, 8), :] - st[0, c, pl.ds(r - 1, 8), :])
            st[1, c, pl.ds(r, 8), :] = new
            st[2, c, pl.ds(r, 8), :] = v - rate * new - e_ref[c, pl.ds(r, 8), :]


def fine_run(st, e_ref, q):
    for first, blocks in ((0, 8), (2, 7), (4, 6), (6, 5)):
        def one(s, carry, first=first, blocks=blocks):
            fine_step(st, e_ref, q, 10 + 2 * (first + s), blocks)
            return carry

        lax.fori_loop(0, 2, one, 0)


def restrict(ref, first):
    total = None
    for j in range(4):
        for c in range(4):
            part = ref[c, pl.ds(first + j, 8, stride=4), :]
            total = part if total is None else total + part
    return total


def kernel(initial, rotation, flips, out, xin, rin, own, own_q, halo, halo_q, fine, fine_q, fine_e, first_run, halo_f,
           rates, rate_own, rate_ring, start_own, start_ring, ring, ring_e, total, anchor_old, work, term_own, term_ring,
           powers, power_in, fine_out, load_sem, send_sem, halo_sem, ring_sem, power_sem, near_sem):
    k = lax.axis_index("tm")
    t = lax.axis_index("tile")
    lane = lax.broadcasted_iota(jnp.int32, (8, 128), 1)
    turned = 127 - lane

    def tile_at(o):
        return lax.rem(t + (o + NT), NT)

    load_x = pltpu.make_async_copy(initial, xin, load_sem.at[0])
    load_q = pltpu.make_async_copy(rotation, rin, load_sem.at[1])
    load_x.start()
    load_q.start()

    at_xh, at_z = k // NZ, lax.rem(k, NZ)
    at_xl, at_y, at_core = t // 8, lax.rem(t // 2, 4), lax.rem(t, 2)

    def place(dx=0, dy=0, dz=0, dc=0):
        px = lax.rem(2 * at_xh + at_xl + (dx + 4), 4)
        return (
            (px // 2) * NZ + lax.rem(at_z + (dz + NZ), NZ),
            lax.rem(px, 2) * 8 + lax.rem(at_y + (dy + 4), 4) * 2 + lax.rem(at_core + dc, 2),
        )

    def meet(sem, *where):
        for there in where:
            pl.semaphore_signal(sem, inc=1, device_id=there, device_id_type=MESH)

    barrier = pltpu.get_barrier_semaphore()
    beside = (place(dy=1), place(dy=-1), place(dx=1), place(dx=-1), place(dz=1), place(dz=-1))
    meet(barrier, (k, tile_at(1)), (k, tile_at(-1)), *beside)

    odd = {0: None}
    up = down = jnp.int32(0)
    for o in range(1, NT // 2 + 1):
        up = up + jnp.where(flips[tile_at(o)] != 0, 1, 0)
        down = down + jnp.where(flips[tile_at(1 - o)] != 0, 1, 0)
        odd[o] = (jnp.zeros((8, 128), jnp.int32) + lax.rem(up, 2)) != 0
        odd[-o] = (jnp.zeros((8, 128), jnp.int32) + lax.rem(down, 2)) != 0

    def turn(x, o, negate, other=None):
        if o == 0:
            return x
        back = gather(x if other is None else other, turned)
        return jnp.where(odd[o], -back if negate else back, x)

    def oriented(src, o):
        return [turn(src[f], o, f == 2) for f in range(3)]

    zero = jnp.zeros((8, 128), jnp.float32)
    for f in range(3):
        for b in range(CR // 8):
            work[f, 8 * b : 8 * b + 8, :] = zero
        for b in (0, 1, CR // 8 - 2, CR // 8 - 1):
            ring[f, 8 * b : 8 * b + 8, :] = zero
        for c in range(4):
            for b in (0, FR // 8 - 2, FR // 8 - 1):
                fine[f, c, 8 * b : 8 * b + 8, :] = zero
        total[f] = jnp.zeros((16, 128), jnp.float32)
    for b in (0, 1, CR // 8 - 2, CR // 8 - 1):
        rates[8 * b : 8 * b + 8, :] = zero
    for c in range(4):
        for b in (0, FR // 8 - 2, FR // 8 - 1):
            fine_q[c, 8 * b : 8 * b + 8, :] = zero

    quarter = lane // 32
    apart = 4 * lax.rem(lane, 32)

    def spread(load, store):
        x = [load(s) for s in range(4)]
        for c in range(4):
            y = [gather(x[s], apart + c) for s in range(4)]
            store(c, jnp.where(quarter < 2, jnp.where(quarter == 0, y[0], y[1]), jnp.where(quarter == 2, y[2], y[3])))

    load_q.wait()
    for b in range(4):
        def store_q(c, x, b=b):
            own_q[c, 8 * b : 8 * b + 8, :] = x
            fine_q[c, FC + 8 * b : FC + 8 * b + 8, :] = x

        spread(lambda s, b=b: rin[8 * b : 8 * b + 8, 128 * s : 128 * s + 128], store_q)
    load_x.wait()
    for f in range(3):
        for b in range(4):
            def store_x(c, x, f=f, b=b):
                own[f, c, 8 * b : 8 * b + 8, :] = x
                fine[f, c, FC + 8 * b : FC + 8 * b + 8, :] = x

            spread(lambda s, f=f, b=b: xin[f, 8 * b : 8 * b + 8, 128 * s : 128 * s + 128], store_x)

    pl.semaphore_wait(barrier, 8)

    def send(src, dst, recv, where, group=0):
        pltpu.make_async_remote_copy(
            src_ref=src, dst_ref=dst, send_sem=send_sem.at[group], recv_sem=recv, device_id=where, device_id_type=MESH
        ).start()

    def take(ref, sem):
        pltpu.make_async_copy(ref, ref, sem).wait()

    send(own.at[:, :, pl.ds(16, 16), :], halo.at[0], halo_sem.at[0], (k, tile_at(1)))
    send(own.at[:, :, pl.ds(0, 16), :], halo.at[1], halo_sem.at[1], (k, tile_at(-1)))
    send(own_q.at[:, pl.ds(16, 16), :], halo_q.at[0], halo_sem.at[2], (k, tile_at(1)))
    send(own_q.at[:, pl.ds(0, 16), :], halo_q.at[1], halo_sem.at[3], (k, tile_at(-1)))
    meet(near_sem.at[0], place(dc=1), *beside)
    rate_own[...] = restrict(own_q, 0) * 0.25
    pl.semaphore_wait(near_sem.at[0], 7)
    meet(near_sem.at[1], place(dy=2), place(dc=1), place(dx=2), place(dz=2), place(dz=-2))

    first_blocks = (k + 3) // 4
    last_blocks = (NK + 2 - k) // 4
    rate_blocks = jnp.maximum(first_blocks, last_blocks)

    def share(src, landing, sems, blocks, group):
        for dx, dy, dc in OTHERS:
            there = lax.rem(at_xl + dx, 2) * 8 + lax.rem(at_y + dy, 4) * 2 + lax.rem(at_core + dc, 2)
            delta = lax.rem(there - t + NT, NT)
            far = jnp.minimum(delta, NT - delta)
            slot = 2 * (far - 1) + jnp.where(delta < 8, 1, 0)

            @pl.when((far - 1) // 2 < blocks)
            def _(there=there, far=far, slot=slot):
                send(src, landing.at[slot], sems.at[(far - 1) // 2], (k, there), group)

    def block(landing, b):
        return landing.at[pl.ds(4 * b, min(4, NT - 1 - 4 * b))]

    def arrive(landing, sems, blocks, use):
        for b in range(4):
            @pl.when(b < blocks)
            def _(b=b):
                take(block(landing, b), sems.at[b])
                for a in (2 * b + 1, 2 * b + 2):
                    use(a, landing.at[2 * a - 2])
                    use(-a, landing.at[2 * a - 2 + (a < NT // 2)])

    def all_sent(landing, group, blocks):
        for b in range(4):
            @pl.when(b < blocks)
            def _(b=b):
                take(block(landing, b), send_sem.at[group])

    take(halo_q.at[0], halo_sem.at[2])
    take(halo_q.at[1], halo_sem.at[3])
    for side, o, row in ((0, -1, FC - 16), (1, 1, FC + 32)):
        for b in range(2):
            for c in range(4):
                x, y = (halo_q[side, cc, 8 * b : 8 * b + 8, :] for cc in (c, 3 - c))
                fine_q[c, row + 8 * b : row + 8 * b + 8, :] = turn(x, o, True, y)

    def fill_rims(src, sem):
        for side, o, row in ((0, -1, FC - 16), (1, 1, FC + 32)):
            take(src.at[side], sem.at[side])
            for f in range(3):
                for b in range(2):
                    for c in range(4):
                        x, y = (src[side, f, cc, 8 * b : 8 * b + 8, :] for cc in (c, 3 - c))
                        fine[f, c, row + 8 * b : row + 8 * b + 8, :] = turn(x, o, f == 2, y)

    fill_rims(halo, halo_sem)
    pl.semaphore_wait(near_sem.at[1], 5)
    meet(near_sem.at[2], place(dx=2))
    share(rate_own, rate_ring, ring_sem.at[0], rate_blocks, 0)
    for f in range(3):
        for half in range(2):
            work[f, pl.ds(CC - 4 + 8 * half, 8), :] = restrict(fine.at[f], FC - 16 + 32 * half) * 0.0625
        anchor_old[f] = work[f, pl.ds(CC, 8), :]
    fine_run(fine, fine_e, fine_q)
    for f in range(3):
        start = restrict(fine.at[f], FC) * 0.0625 - anchor_old[f]
        start_own[f] = start
        ring[f, CC : CC + 8, :] = start
    share(start_own, start_ring, ring_sem.at[1], first_blocks, 1)
    for f in range(3):
        for c in range(4):
            first_run[f, c] = fine[f, c, FC : FC + 32, :]
    send(first_run.at[:, :, pl.ds(16, 16), :], halo_f.at[0], halo_sem.at[4], (k, tile_at(1)))
    send(first_run.at[:, :, pl.ds(0, 16), :], halo_f.at[1], halo_sem.at[5], (k, tile_at(-1)))

    rates[CC : CC + 8, :] = rate_own[...]

    def use_rate(o, ref):
        rates[CC + 8 * o : CC + 8 * o + 8, :] = turn(ref[...], o, True)

    arrive(rate_ring, ring_sem.at[0], rate_blocks, use_rate)
    coarse(work, ring_e, rates, CC, 8)
    for f in range(3):
        anchor_old[f] = work[f, CC : CC + 8, :]

    def use_in(whole):
        def use(o, ref):
            for f, x in enumerate(oriented(ref, o)):
                whole[f, CC + 8 * o : CC + 8 * o + 8, :] = x

        return use

    arrive(start_ring, ring_sem.at[1], first_blocks, use_in(ring))

    for m in (3, 2, 1, 0):
        def chain(s, carry, m=m):
            coarse(ring, ring_e, rates, CC - 16 - 16 * m, 40 + 32 * m)
            for f in range(3):
                total[f] = total[f] + ring[f, pl.ds(CC - 4, 16), :]
            return carry

        lax.fori_loop(0, jnp.clip(k - 1 - 4 * m, 0, 4), chain, 0)

    fill_rims(halo_f, halo_sem.at[pl.ds(4, 2)])

    for f in range(3):
        more = total[f]
        for c in range(4):
            for j in range(4):
                rows = pl.ds(FC - 16 + j, 16, stride=4)
                fine[f, c, rows, :] = fine[f, c, rows, :] + more
    coarse(ring, ring_e, rates, CC, 8)
    for f in range(3):
        anchor_old[f] = anchor_old[f] + total[f, pl.ds(4, 8), :] + ring[f, CC : CC + 8, :]
    fine_run(fine, fine_e, fine_q)

    @pl.when(k == 0)
    def _():
        for f in range(3):
            anchor_old[f] = zero
            for c in range(4):
                fine[f, c, FC : FC + 32, :] = first_run[f, c]

    for f in range(3):
        mean = restrict(fine.at[f], FC) * 0.0625
        start_own_f = mean - anchor_old[f]
        total[f, 0:8, :] = mean
        term_own[f] = start_own_f

    share(term_own, term_ring, ring_sem.at[2], last_blocks, 2)

    apart_out = lane // 4
    phase = lax.rem(lane, 4)
    for f in range(3):
        for b in range(4):
            x = [fine[f, c, FC + 8 * b : FC + 8 * b + 8, :] for c in range(4)]
            for s in range(4):
                y = [gather(x[c], apart_out + 32 * s) for c in range(4)]
                fine_out[f, s, 8 * b : 8 * b + 8, :] = jnp.where(
                    phase < 2, jnp.where(phase == 0, y[0], y[1]), jnp.where(phase == 2, y[2], y[3])
                )

    for f in range(3):
        work[f, CC : CC + 8, :] = term_own[f]
    arrive(term_ring, ring_sem.at[2], last_blocks, use_in(work))
    pl.semaphore_wait(near_sem.at[2], 1)

    last = NK - 1 - k
    m = jnp.int32(0)
    for group in (3, 2, 1, 0):
        def power(s, m, group=group):
            coarse(work, ring_e, rates, CC - 12 - 16 * group, 32 + 32 * group)
            powers[m] = work[:, CC : CC + 8, :]
            send(powers.at[m], power_in.at[m], power_sem.at[m], (k + m + 1, t), 3)
            return m + 1

        m = lax.fori_loop(0, jnp.clip(last - 4 * group, 0, 4), power, m)

    def add(m, carry):
        take(power_in.at[m], power_sem.at[m])
        term_own[...] = term_own[...] + power_in[m]
        return carry

    all_sent(term_ring, 2, last_blocks)
    lax.fori_loop(0, k, add, 0)

    for f in range(3):
        extra = term_own[f] - total[f, 0:8, :]
        for s in range(4):
            more = gather(extra, apart_out + 32 * s)
            for j in range(4):
                rows = pl.ds(j, 8, stride=4)
                fine_out[f, s, rows, :] = fine_out[f, s, rows, :] + more
            out[0, f, :, 128 * s : 128 * s + 128] = fine_out[f, s]

    for _ in range(2):
        take(halo, send_sem.at[0])
    take(halo_q, send_sem.at[0])
    all_sent(rate_ring, 0, rate_blocks)
    all_sent(start_ring, 1, first_blocks)

    def sent(m, carry):
        take(powers.at[m], send_sem.at[3])
        return carry

    lax.fori_loop(0, last, sent, 0)


def body(initial, rotation, seam_flip):
    def vmem(*shape):
        return pltpu.VMEM(shape, jnp.float32)

    dma = pltpu.SemaphoreType.DMA
    scratch = [
        vmem(3, 32, 512), vmem(32, 512),
        vmem(3, 4, 32, 128), vmem(4, 32, 128),
        vmem(2, 3, 4, 16, 128), vmem(2, 4, 16, 128),
        vmem(3, 4, FR, 128), vmem(4, FR, 128), vmem(4, FR, 128),
        vmem(3, 4, 32, 128), vmem(2, 3, 4, 16, 128),
        vmem(CR, 128), vmem(8, 128), vmem(NT - 1, 8, 128),
        vmem(3, 8, 128), vmem(NT - 1, 3, 8, 128),
        vmem(3, CR, 128), vmem(CR, 128),
        vmem(3, 16, 128), vmem(3, 8, 128),
        vmem(3, CR, 128),
        vmem(3, 8, 128), vmem(NT - 1, 3, 8, 128),
        vmem(NK - 1, 3, 8, 128), vmem(NK - 1, 3, 8, 128),
        vmem(3, 4, 32, 128),
        dma((2,)), dma((4,)), dma((6,)), dma((3, 4)), dma((NK - 1,)), pltpu.SemaphoreType.REGULAR((3,)),
    ]
    return pl.pallas_call(
        kernel,
        out_shape=jax.ShapeDtypeStruct((1, 3, 32, 512), jnp.float32),
        in_specs=[
            pl.BlockSpec(memory_space=pl.ANY),
            pl.BlockSpec(memory_space=pl.ANY),
            pl.BlockSpec(memory_space=pltpu.SMEM),
        ],
        out_specs=pl.BlockSpec(memory_space=pltpu.VMEM),
        scratch_shapes=scratch,
        compiler_params=pltpu.CompilerParams(
            collective_id=0, has_side_effects=True, vmem_limit_bytes=60 * 1024 * 1024
        ),
        name="parareal",
    )(initial, rotation, seam_flip)


def solution(mesh):
    in_specs = (P(None, "tile", None), P("tile", None), P())
    out_specs = P("tm", None, "tile", None)
    return jax.shard_map(body, mesh=mesh, in_specs=in_specs, out_specs=out_specs, check_vma=False)
```

```python
import jax
import jax.numpy as jnp
from jax import lax
from jax.experimental import pallas as pl
from jax.experimental.pallas import tpu as pltpu
from jax.sharding import PartitionSpec as P

MESH = pl.DeviceIdType.MESH
NT = 16
NK = 16
HC = 0.45
FC = 24
FR = 88
CC = 80
CR = 168
NZ = 8
OTHERS = tuple((x, y, c) for y in (2, 1, 3, 0) for x in (1, 0) for c in (1, 0) if (x, y, c) != (0, 0, 0))


def gather(x, idx):
    return jnp.take_along_axis(x, idx, axis=1)


def ahead(x):
    return pltpu.roll(x, 127, 1)


def behind(x):
    return pltpu.roll(x, 1, 1)


def blocks(first, past):
    return range(first // 8 * 8, -(-past // 8) * 8, 8)


def coarse_step(st, e_ref, q, first, past):
    for r in blocks(first - 1, past + 1):
        g = st[0, r : r + 8, :] - HC * (st[1, r + 1 : r + 9, :] - st[1, r - 1 : r + 7, :])
        v = st[2, r : r + 8, :]
        wide = pltpu.roll(v, 126, 1) - 2.0 * v + pltpu.roll(v, 2, 1)
        st[0, r : r + 8, :] = g - HC * (ahead(v) - behind(v))
        e_ref[r : r + 8, :] = HC * ((ahead(g) - behind(g)) - HC * wide)
    for r in blocks(first, past):
        u, v, rate = st[1, r : r + 8, :], st[2, r : r + 8, :], q[r : r + 8, :]
        new = u + rate * v - HC * (st[0, r + 1 : r + 9, :] - st[0, r - 1 : r + 7, :])
        st[1, r : r + 8, :] = new
        st[2, r : r + 8, :] = v - rate * new - e_ref[r : r + 8, :]


def coarse(st, e_ref, q, first, past):
    coarse_step(st, e_ref, q, first - 2, past + 2)
    coarse_step(st, e_ref, q, first, past)


def fine_step(st, e_ref, q, first, past):
    for r in blocks(first - 1, past + 1):
        v = [st[2, c, r : r + 8, :] for c in range(4)]
        g = [st[0, c, r : r + 8, :] - HC * (st[1, c, r + 1 : r + 9, :] - st[1, c, r - 1 : r + 7, :]) for c in range(4)]
        vs = [behind(v[2]), behind(v[3])] + v + [ahead(v[0]), ahead(v[1])]
        gs = [behind(g[3])] + g + [ahead(g[0])]
        for c in range(4):
            st[0, c, r : r + 8, :] = g[c] - HC * (vs[c + 3] - vs[c + 1])
            e_ref[c, r : r + 8, :] = HC * ((gs[c + 2] - gs[c]) - HC * (vs[c + 4] - 2.0 * v[c] + vs[c]))
    for r in blocks(first, past):
        for c in range(4):
            u, v, rate = st[1, c, r : r + 8, :], st[2, c, r : r + 8, :], q[c, r : r + 8, :]
            new = u + rate * v - HC * (st[0, c, r + 1 : r + 9, :] - st[0, c, r - 1 : r + 7, :])
            st[1, c, r : r + 8, :] = new
            st[2, c, r : r + 8, :] = v - rate * new - e_ref[c, r : r + 8, :]


def fine_run(st, e_ref, q):
    for s in range(8):
        fine_step(st, e_ref, q, FC - 14 + 2 * s, FC + 46 - 2 * s)


def restrict(ref, first):
    total = None
    for j in range(4):
        for c in range(4):
            part = ref[c, pl.ds(first + j, 8, stride=4), :]
            total = part if total is None else total + part
    return total


def kernel(initial, rotation, flips, out, xin, rin, own, own_q, halo, halo_q, fine, fine_q, fine_e, first_run, halo_f,
           rates, rate_own, rate_ring, start_own, start_ring, ring, ring_e, total, total_j, total_k, first_end, work, term_own, term_ring,
           powers, power_in, fine_out, load_sem, send_sem, halo_sem, ring_sem, power_sem, near_sem):
    k = lax.axis_index("tm")
    t = lax.axis_index("tile")
    lane = lax.broadcasted_iota(jnp.int32, (8, 128), 1)
    turned = 127 - lane

    def tile_at(o):
        return lax.rem(t + (o + NT), NT)

    load_x = pltpu.make_async_copy(initial, xin, load_sem.at[0])
    load_q = pltpu.make_async_copy(rotation, rin, load_sem.at[1])
    load_x.start()
    load_q.start()

    at_xh, at_z = k // NZ, lax.rem(k, NZ)
    at_xl, at_y, at_core = t // 8, lax.rem(t // 2, 4), lax.rem(t, 2)

    def place(dx=0, dy=0, dz=0, dc=0):
        px = lax.rem(2 * at_xh + at_xl + (dx + 4), 4)
        return (
            (px // 2) * NZ + lax.rem(at_z + (dz + NZ), NZ),
            lax.rem(px, 2) * 8 + lax.rem(at_y + (dy + 4), 4) * 2 + lax.rem(at_core + dc, 2),
        )

    def meet(sem, *where):
        for there in where:
            pl.semaphore_signal(sem, inc=1, device_id=there, device_id_type=MESH)

    barrier = pltpu.get_barrier_semaphore()
    meet(barrier, *((k, tile_at(o)) for o in (1, -1, 8, 4, -4, 2, -2, 3, -3, 5, -5, 6, -6, 7, -7)), place(dx=2))
    for dz in range(1, NZ):
        @pl.when(at_z + dz < NZ)
        def _(dz=dz):
            meet(barrier, (at_z + dz, t), (NZ + at_z + dz, t))

    j = jnp.where(k < 4, jnp.where(k == 0, 8, k), jnp.where(k < 8, jnp.where(k == 4, 0, k + 4), jnp.where(k < 12, k - 4, k)))
    n = jnp.maximum(j, k)

    odd = {0: None}
    up = down = jnp.int32(0)
    for o in range(1, NT // 2 + 1):
        up = up + jnp.where(flips[tile_at(o)] != 0, 1, 0)
        down = down + jnp.where(flips[tile_at(1 - o)] != 0, 1, 0)
        odd[o] = (jnp.zeros((8, 128), jnp.int32) + lax.rem(up, 2)) != 0
        odd[-o] = (jnp.zeros((8, 128), jnp.int32) + lax.rem(down, 2)) != 0

    def turn(x, o, negate, other=None):
        if o == 0:
            return x
        back = gather(x if other is None else other, turned)
        return jnp.where(odd[o], -back if negate else back, x)

    def oriented(src, o):
        return [turn(src[f], o, f == 2) for f in range(3)]

    zero = jnp.zeros((8, 128), jnp.float32)
    for f in range(3):
        for b in range(CR // 8):
            work[f, 8 * b : 8 * b + 8, :] = zero
        for b in (0, 1, CR // 8 - 2, CR // 8 - 1):
            ring[f, 8 * b : 8 * b + 8, :] = zero
        for c in range(4):
            for b in (0, FR // 8 - 2, FR // 8 - 1):
                fine[f, c, 8 * b : 8 * b + 8, :] = zero
        for ref in (total, total_j, total_k):
            ref[f] = jnp.zeros((16, 128), jnp.float32)
    for b in (0, 1, CR // 8 - 2, CR // 8 - 1):
        rates[8 * b : 8 * b + 8, :] = zero
    for c in range(4):
        for b in (0, FR // 8 - 2, FR // 8 - 1):
            fine_q[c, 8 * b : 8 * b + 8, :] = zero

    quarter = lane // 32
    apart = 4 * lax.rem(lane, 32)

    def spread(load, store):
        x = [load(s) for s in range(4)]
        for c in range(4):
            y = [gather(x[s], apart + c) for s in range(4)]
            store(c, jnp.where(quarter < 2, jnp.where(quarter == 0, y[0], y[1]), jnp.where(quarter == 2, y[2], y[3])))

    load_q.wait()
    for b in range(4):
        def store_q(c, x, b=b):
            own_q[c, 8 * b : 8 * b + 8, :] = x
            fine_q[c, FC + 8 * b : FC + 8 * b + 8, :] = x

        spread(lambda s, b=b: rin[8 * b : 8 * b + 8, 128 * s : 128 * s + 128], store_q)
    load_x.wait()
    for f in range(3):
        for b in range(4):
            def store_x(c, x, f=f, b=b):
                own[f, c, 8 * b : 8 * b + 8, :] = x
                fine[f, c, FC + 8 * b : FC + 8 * b + 8, :] = x

            spread(lambda s, f=f, b=b: xin[f, 8 * b : 8 * b + 8, 128 * s : 128 * s + 128], store_x)

    pl.semaphore_wait(barrier, NT + 2 * at_z)

    def send(src, dst, recv, where, group=0):
        pltpu.make_async_remote_copy(
            src_ref=src, dst_ref=dst, send_sem=send_sem.at[group], recv_sem=recv, device_id=where, device_id_type=MESH
        ).start()

    def take(ref, sem):
        pltpu.make_async_copy(ref, ref, sem).wait()

    send(own.at[:, :, pl.ds(16, 16), :], halo.at[0], halo_sem.at[0], (k, tile_at(1)))
    send(own.at[:, :, pl.ds(0, 16), :], halo.at[1], halo_sem.at[1], (k, tile_at(-1)))
    send(own_q.at[:, pl.ds(16, 16), :], halo_q.at[0], halo_sem.at[2], (k, tile_at(1)))
    send(own_q.at[:, pl.ds(0, 16), :], halo_q.at[1], halo_sem.at[3], (k, tile_at(-1)))
    rate_own[...] = restrict(own_q, 0) * 0.25

    first_blocks = (n + 3) // 4
    last_blocks = jnp.where(j == 0, 0, (NK + 2 - j) // 4)
    rate_blocks = jnp.maximum(first_blocks, last_blocks)

    def share(src, landing, sems, count, group):
        for dx, dy, dc in OTHERS:
            there = lax.rem(at_xl + dx, 2) * 8 + lax.rem(at_y + dy, 4) * 2 + lax.rem(at_core + dc, 2)
            delta = lax.rem(there - t + NT, NT)
            far = jnp.minimum(delta, NT - delta)
            slot = 2 * (far - 1) + jnp.where(delta < 8, 1, 0)

            @pl.when((far - 1) // 2 < count)
            def _(there=there, far=far, slot=slot):
                send(src, landing.at[slot], sems.at[(far - 1) // 2], (k, there), group)

    def block(landing, b):
        return landing.at[pl.ds(4 * b, min(4, NT - 1 - 4 * b))]

    def arrive(landing, sems, count, use):
        for b in range(4):
            @pl.when(b < count)
            def _(b=b):
                take(block(landing, b), sems.at[b])
                for a in (2 * b + 1, 2 * b + 2):
                    use(a, landing.at[2 * a - 2])
                    use(-a, landing.at[2 * a - 2 + (a < NT // 2)])

    def all_sent(landing, group, count):
        for b in range(4):
            @pl.when(b < count)
            def _(b=b):
                take(block(landing, b), send_sem.at[group])

    for dz in range(1, NZ):
        @pl.when(at_z >= dz)
        def _(dz=dz):
            meet(near_sem, (at_z - dz, t), (NZ + at_z - dz, t))

    take(halo_q.at[0], halo_sem.at[2])
    take(halo_q.at[1], halo_sem.at[3])
    for side, o, row in ((0, -1, FC - 16), (1, 1, FC + 32)):
        for b in range(2):
            for c in range(4):
                x, y = (halo_q[side, cc, 8 * b : 8 * b + 8, :] for cc in (c, 3 - c))
                fine_q[c, row + 8 * b : row + 8 * b + 8, :] = turn(x, o, True, y)

    def fill_rims(src, sem):
        for side, o, row in ((0, -1, FC - 16), (1, 1, FC + 32)):
            take(src.at[side], sem.at[side])
            for f in range(3):
                for b in range(2):
                    for c in range(4):
                        x, y = (src[side, f, cc, 8 * b : 8 * b + 8, :] for cc in (c, 3 - c))
                        fine[f, c, row + 8 * b : row + 8 * b + 8, :] = turn(x, o, f == 2, y)

    fill_rims(halo, halo_sem)
    share(rate_own, rate_ring, ring_sem.at[0], rate_blocks, 0)
    fine_run(fine, fine_e, fine_q)
    for f in range(3):
        first_end[f] = restrict(fine.at[f], FC) * 0.0625
        start = first_end[f] - restrict(own.at[f], 0) * 0.0625
        start_own[f] = start
        ring[f, CC : CC + 8, :] = start
        for c in range(4):
            first_run[f, c] = fine[f, c, FC : FC + 32, :]

    def edges():
        send(first_run.at[:, :, pl.ds(16, 16), :], halo_f.at[0], halo_sem.at[4], (k, tile_at(1)))
        send(first_run.at[:, :, pl.ds(0, 16), :], halo_f.at[1], halo_sem.at[5], (k, tile_at(-1)))

    share(start_own, start_ring, ring_sem.at[1], first_blocks, 1)
    edges()

    rates[CC : CC + 8, :] = rate_own[...]

    def use_rate(o, ref):
        rates[CC + 8 * o : CC + 8 * o + 8, :] = turn(ref[...], o, True)

    arrive(rate_ring, ring_sem.at[0], rate_blocks, use_rate)

    def use_in(whole):
        def use(o, ref):
            for f, x in enumerate(oriented(ref, o)):
                whole[f, CC + 8 * o : CC + 8 * o + 8, :] = x

        return use

    arrive(start_ring, ring_sem.at[1], first_blocks, use_in(ring))

    def chain(least, most, i):
        for m in (3, 2, 1, 0):
            def one(_, i, m=m):
                coarse(ring, ring_e, rates, CC - 12 - 16 * m, CC + 20 + 16 * m)
                for f in range(3):
                    total[f] = total[f] + ring[f, pl.ds(CC - 4, 16), :]

                @pl.when(i == j - 1)
                def _():
                    total_j[...] = total[...]

                @pl.when(i == k - 1)
                def _():
                    total_k[...] = total[...]

                return i + 1

            count = jnp.minimum(most, 4 * m + 4) - jnp.maximum(least, 4 * m)
            i = lax.fori_loop(0, jnp.maximum(count, 0), one, i)
        return i

    def fine_from(change):
        for side, o, row in ((0, -1, FC - 16), (1, 1, FC + 32)):
            for f in range(3):
                for b in range(2):
                    for c in range(4):
                        x, y = (halo_f[side, f, cc, 8 * b : 8 * b + 8, :] for cc in (c, 3 - c))
                        fine[f, c, row + 8 * b : row + 8 * b + 8, :] = turn(x, o, f == 2, y)
        for f in range(3):
            more = change[f]
            for c in range(4):
                fine[f, c, FC : FC + 32, :] = first_run[f, c]
                for p in range(4):
                    rows = pl.ds(FC - 16 + p, 16, stride=4)
                    fine[f, c, rows, :] = fine[f, c, rows, :] + more
        fine_run(fine, fine_e, fine_q)

    i = chain(n - j, n, jnp.int32(1))
    take(halo_f.at[0], halo_sem.at[4])
    take(halo_f.at[1], halo_sem.at[5])

    @pl.when(j > 0)
    def _():
        fine_from(total_j)

    for f in range(3):
        term = restrict(fine.at[f], FC) * 0.0625 - (first_end[f] + total[f, 4:12, :])
        term_own[f] = term
        work[f, CC : CC + 8, :] = term
    share(term_own, term_ring, ring_sem.at[2], last_blocks, 2)

    chain(0, n - j, i)

    @pl.when((j != k) & (k > 0))
    def _():
        fine_from(total_k)

    @pl.when(k == 0)
    def _():
        for f in range(3):
            for c in range(4):
                fine[f, c, FC : FC + 32, :] = first_run[f, c]


    apart_out = lane // 4
    phase = lax.rem(lane, 4)
    for f in range(3):
        for b in range(4):
            x = [fine[f, c, FC + 8 * b : FC + 8 * b + 8, :] for c in range(4)]
            for s in range(4):
                y = [gather(x[c], apart_out + 32 * s) for c in range(4)]
                fine_out[f, s, 8 * b : 8 * b + 8, :] = jnp.where(
                    phase < 2, jnp.where(phase == 0, y[0], y[1]), jnp.where(phase == 2, y[2], y[3])
                )

    arrive(term_ring, ring_sem.at[2], last_blocks, use_in(work))

    @pl.when(at_z < NZ - 1)
    def _():
        pl.semaphore_wait(near_sem, 2 * (NZ - 1 - at_z))


    last = jnp.where(j == 0, 0, NK - 1 - j)
    m = jnp.int32(0)
    for group in (3, 2, 1, 0):
        def power(s, m, group=group):
            coarse(work, ring_e, rates, CC - 12 - 16 * group, CC + 20 + 16 * group)
            powers[m] = work[:, CC : CC + 8, :]

            @pl.when(j + m + 1 != k)
            def _():
                send(powers.at[m], power_in.at[m], power_sem.at[m], (j + m + 1, t), 3)

            @pl.when(j + m + 1 == k)
            def _():
                pltpu.make_async_copy(powers.at[m], power_in.at[m], power_sem.at[m]).start()

            return m + 1

        m = lax.fori_loop(0, jnp.clip(last - 4 * group, 0, 4), power, m)

    all_sent(term_ring, 2, last_blocks)
    term_own[...] = jnp.zeros((3, 8, 128), jnp.float32)

    def add(m, carry):
        take(power_in.at[m], power_sem.at[m])
        term_own[...] = term_own[...] + power_in[m]
        return carry

    lax.fori_loop(0, k - 1, add, 0)

    for f in range(3):
        extra = term_own[f]
        for s in range(4):
            more = gather(extra, apart_out + 32 * s)
            for p in range(4):
                rows = pl.ds(p, 8, stride=4)
                fine_out[f, s, rows, :] = fine_out[f, s, rows, :] + more
            out[0, f, :, 128 * s : 128 * s + 128] = fine_out[f, s]

    for _ in range(2):
        take(halo, send_sem.at[0])
    take(halo_q, send_sem.at[0])
    all_sent(rate_ring, 0, rate_blocks)
    all_sent(start_ring, 1, first_blocks)

    def sent(m, carry):
        take(powers.at[m], send_sem.at[3])
        return carry

    lax.fori_loop(0, last - jnp.where((j > 0) & (k > j), 1, 0), sent, 0)


def body(initial, rotation, seam_flip):
    def vmem(*shape):
        return pltpu.VMEM(shape, jnp.float32)

    dma = pltpu.SemaphoreType.DMA
    scratch = [
        vmem(3, 32, 512), vmem(32, 512),
        vmem(3, 4, 32, 128), vmem(4, 32, 128),
        vmem(2, 3, 4, 16, 128), vmem(2, 4, 16, 128),
        vmem(3, 4, FR, 128), vmem(4, FR, 128), vmem(4, FR, 128),
        vmem(3, 4, 32, 128), vmem(2, 3, 4, 16, 128),
        vmem(CR, 128), vmem(8, 128), vmem(NT - 1, 8, 128),
        vmem(3, 8, 128), vmem(NT - 1, 3, 8, 128),
        vmem(3, CR, 128), vmem(CR, 128),
        vmem(3, 16, 128), vmem(3, 16, 128), vmem(3, 16, 128), vmem(3, 8, 128),
        vmem(3, CR, 128),
        vmem(3, 8, 128), vmem(NT - 1, 3, 8, 128),
        vmem(NK - 1, 3, 8, 128), vmem(NK - 1, 3, 8, 128),
        vmem(3, 4, 32, 128),
        dma((2,)), dma((4,)), dma((6,)), dma((3, 4)), dma((NK - 1,)), pltpu.SemaphoreType.REGULAR,
    ]
    return pl.pallas_call(
        kernel,
        out_shape=jax.ShapeDtypeStruct((1, 3, 32, 512), jnp.float32),
        in_specs=[
            pl.BlockSpec(memory_space=pl.ANY),
            pl.BlockSpec(memory_space=pl.ANY),
            pl.BlockSpec(memory_space=pltpu.SMEM),
        ],
        out_specs=pl.BlockSpec(memory_space=pltpu.VMEM),
        scratch_shapes=scratch,
        compiler_params=pltpu.CompilerParams(
            collective_id=0, has_side_effects=True, vmem_limit_bytes=60 * 1024 * 1024
        ),
        name="parareal",
    )(initial, rotation, seam_flip)


def solution(mesh):
    in_specs = (P(None, "tile", None), P("tile", None), P())
    out_specs = P("tm", None, "tile", None)
    return jax.shard_map(body, mesh=mesh, in_specs=in_specs, out_specs=out_specs, check_vma=False)
```

```python
import jax
import jax.numpy as jnp
from jax import lax
from jax.experimental import pallas as pl
from jax.experimental.pallas import tpu as pltpu
from jax.sharding import PartitionSpec as P

MESH = pl.DeviceIdType.MESH
NT = 16
NK = 16
HC = 0.45
FC = 24
FR = 88
CC = 80
CR = 168
NZ = 8
OTHERS = tuple((x, y, c) for y in (2, 1, 3, 0) for x in (1, 0) for c in (1, 0) if (x, y, c) != (0, 0, 0))


def gather(x, idx):
    return jnp.take_along_axis(x, idx, axis=1)


def ahead(x):
    return pltpu.roll(x, 127, 1)


def behind(x):
    return pltpu.roll(x, 1, 1)


def blocks(first, past):
    return range(first // 8 * 8, -(-past // 8) * 8, 8)


def coarse_step(st, e_ref, q, first, past):
    for r in blocks(first - 1, past + 1):
        g = st[0, r : r + 8, :] - HC * (st[1, r + 1 : r + 9, :] - st[1, r - 1 : r + 7, :])
        v = st[2, r : r + 8, :]
        wide = pltpu.roll(v, 126, 1) - 2.0 * v + pltpu.roll(v, 2, 1)
        st[0, r : r + 8, :] = g - HC * (ahead(v) - behind(v))
        e_ref[r : r + 8, :] = HC * ((ahead(g) - behind(g)) - HC * wide)
    for r in blocks(first, past):
        u, v, rate = st[1, r : r + 8, :], st[2, r : r + 8, :], q[r : r + 8, :]
        new = u + rate * v - HC * (st[0, r + 1 : r + 9, :] - st[0, r - 1 : r + 7, :])
        st[1, r : r + 8, :] = new
        st[2, r : r + 8, :] = v - rate * new - e_ref[r : r + 8, :]


def coarse(st, e_ref, q, first, past):
    coarse_step(st, e_ref, q, first - 2, past + 2)
    coarse_step(st, e_ref, q, first, past)


def fine_step(st, e_ref, q, first, past):
    for r in blocks(first - 1, past + 1):
        v = [st[2, c, r : r + 8, :] for c in range(4)]
        g = [st[0, c, r : r + 8, :] - HC * (st[1, c, r + 1 : r + 9, :] - st[1, c, r - 1 : r + 7, :]) for c in range(4)]
        vs = [behind(v[2]), behind(v[3])] + v + [ahead(v[0]), ahead(v[1])]
        gs = [behind(g[3])] + g + [ahead(g[0])]
        for c in range(4):
            st[0, c, r : r + 8, :] = g[c] - HC * (vs[c + 3] - vs[c + 1])
            e_ref[c, r : r + 8, :] = HC * ((gs[c + 2] - gs[c]) - HC * (vs[c + 4] - 2.0 * v[c] + vs[c]))
    for r in blocks(first, past):
        for c in range(4):
            u, v, rate = st[1, c, r : r + 8, :], st[2, c, r : r + 8, :], q[c, r : r + 8, :]
            new = u + rate * v - HC * (st[0, c, r + 1 : r + 9, :] - st[0, c, r - 1 : r + 7, :])
            st[1, c, r : r + 8, :] = new
            st[2, c, r : r + 8, :] = v - rate * new - e_ref[c, r : r + 8, :]


def fine_run(st, e_ref, q):
    for s in range(8):
        fine_step(st, e_ref, q, FC - 14 + 2 * s, FC + 46 - 2 * s)


def restrict(ref, first):
    total = None
    for j in range(4):
        for c in range(4):
            part = ref[c, pl.ds(first + j, 8, stride=4), :]
            total = part if total is None else total + part
    return total


def kernel(initial, rotation, flips, out, change, xin, rin, own, own_q, halo, halo_q, fine, fine_q, fine_e, first_run, halo_f,
           rates, rate_own, rate_ring, start_own, start_ring, ring, ring_e, total, total_j, total_k, first_end, work, term_own, term_ring,
           powers, power_in, fine_out, load_sem, send_sem, halo_sem, ring_sem, power_sem, near_sem):
    k = lax.axis_index("tm")
    t = lax.axis_index("tile")
    lane = lax.broadcasted_iota(jnp.int32, (8, 128), 1)
    turned = 127 - lane

    def tile_at(o):
        return lax.rem(t + (o + NT), NT)

    load_x = pltpu.make_async_copy(initial, xin, load_sem.at[0])
    load_q = pltpu.make_async_copy(rotation, rin, load_sem.at[1])
    load_x.start()
    load_q.start()

    at_xh, at_z = k // NZ, lax.rem(k, NZ)
    at_xl, at_y, at_core = t // 8, lax.rem(t // 2, 4), lax.rem(t, 2)

    def place(dx=0, dy=0, dz=0, dc=0):
        px = lax.rem(2 * at_xh + at_xl + (dx + 4), 4)
        return (
            (px // 2) * NZ + lax.rem(at_z + (dz + NZ), NZ),
            lax.rem(px, 2) * 8 + lax.rem(at_y + (dy + 4), 4) * 2 + lax.rem(at_core + dc, 2),
        )

    def meet(sem, *where):
        for there in where:
            pl.semaphore_signal(sem, inc=1, device_id=there, device_id_type=MESH)

    barrier = pltpu.get_barrier_semaphore()
    meet(barrier, *((k, tile_at(o)) for o in (1, -1, 8, 4, -4, 2, -2, 3, -3, 5, -5, 6, -6, 7, -7)), place(dx=2))
    for dz in range(1, NZ):
        @pl.when(at_z + dz < NZ)
        def _(dz=dz):
            meet(barrier, (at_z + dz, t), (NZ + at_z + dz, t))

    j = jnp.where(k < 4, jnp.where(k == 0, 8, k), jnp.where(k < 8, k + 8, jnp.where(k < 12, k - 4, k - 3)))
    j = jnp.where(k == 7, 0, jnp.where(k == 15, 15, j))
    n = jnp.maximum(j, k)

    odd = {0: None}
    up = down = jnp.int32(0)
    for o in range(1, NT // 2 + 1):
        up = up + jnp.where(flips[tile_at(o)] != 0, 1, 0)
        down = down + jnp.where(flips[tile_at(1 - o)] != 0, 1, 0)
        odd[o] = (jnp.zeros((8, 128), jnp.int32) + lax.rem(up, 2)) != 0
        odd[-o] = (jnp.zeros((8, 128), jnp.int32) + lax.rem(down, 2)) != 0

    def turn(x, o, negate, other=None):
        if o == 0:
            return x
        back = gather(x if other is None else other, turned)
        return jnp.where(odd[o], -back if negate else back, x)

    def oriented(src, o):
        return [turn(src[f], o, f == 2) for f in range(3)]

    zero = jnp.zeros((8, 128), jnp.float32)
    for f in range(3):
        for b in range(CR // 8):
            work[f, 8 * b : 8 * b + 8, :] = zero
        for b in (0, 1, CR // 8 - 2, CR // 8 - 1):
            ring[f, 8 * b : 8 * b + 8, :] = zero
        for c in range(4):
            for b in (0, FR // 8 - 2, FR // 8 - 1):
                fine[f, c, 8 * b : 8 * b + 8, :] = zero
        for ref in (total, total_j, total_k):
            ref[f] = jnp.zeros((16, 128), jnp.float32)
    for b in (0, 1, CR // 8 - 2, CR // 8 - 1):
        rates[8 * b : 8 * b + 8, :] = zero
    for c in range(4):
        for b in (0, FR // 8 - 2, FR // 8 - 1):
            fine_q[c, 8 * b : 8 * b + 8, :] = zero

    quarter = lane // 32
    apart = 4 * lax.rem(lane, 32)

    def spread(load, store):
        x = [load(s) for s in range(4)]
        for c in range(4):
            y = [gather(x[s], apart + c) for s in range(4)]
            store(c, jnp.where(quarter < 2, jnp.where(quarter == 0, y[0], y[1]), jnp.where(quarter == 2, y[2], y[3])))

    load_q.wait()
    for b in range(4):
        def store_q(c, x, b=b):
            own_q[c, 8 * b : 8 * b + 8, :] = x
            fine_q[c, FC + 8 * b : FC + 8 * b + 8, :] = x

        spread(lambda s, b=b: rin[8 * b : 8 * b + 8, 128 * s : 128 * s + 128], store_q)
    load_x.wait()
    for f in range(3):
        for b in range(4):
            def store_x(c, x, f=f, b=b):
                own[f, c, 8 * b : 8 * b + 8, :] = x
                fine[f, c, FC + 8 * b : FC + 8 * b + 8, :] = x

            spread(lambda s, f=f, b=b: xin[f, 8 * b : 8 * b + 8, 128 * s : 128 * s + 128], store_x)

    pl.semaphore_wait(barrier, NT + 2 * at_z)

    def send(src, dst, recv, where, group=0):
        pltpu.make_async_remote_copy(
            src_ref=src, dst_ref=dst, send_sem=send_sem.at[group], recv_sem=recv, device_id=where, device_id_type=MESH
        ).start()

    def take(ref, sem):
        pltpu.make_async_copy(ref, ref, sem).wait()

    send(own.at[:, :, pl.ds(16, 16), :], halo.at[0], halo_sem.at[0], (k, tile_at(1)))
    send(own.at[:, :, pl.ds(0, 16), :], halo.at[1], halo_sem.at[1], (k, tile_at(-1)))
    send(own_q.at[:, pl.ds(16, 16), :], halo_q.at[0], halo_sem.at[2], (k, tile_at(1)))
    send(own_q.at[:, pl.ds(0, 16), :], halo_q.at[1], halo_sem.at[3], (k, tile_at(-1)))
    rate_own[...] = restrict(own_q, 0) * 0.25

    first_blocks = (n + 3) // 4
    last_blocks = jnp.where(j == 0, 0, (NK + 2 - j) // 4)
    rate_blocks = jnp.maximum(first_blocks, last_blocks)

    def share(src, landing, sems, count, group):
        for dx, dy, dc in OTHERS:
            there = lax.rem(at_xl + dx, 2) * 8 + lax.rem(at_y + dy, 4) * 2 + lax.rem(at_core + dc, 2)
            delta = lax.rem(there - t + NT, NT)
            far = jnp.minimum(delta, NT - delta)
            slot = 2 * (far - 1) + jnp.where(delta < 8, 1, 0)

            @pl.when((far - 1) // 2 < count)
            def _(there=there, far=far, slot=slot):
                send(src, landing.at[slot], sems.at[(far - 1) // 2], (k, there), group)

    def block(landing, b):
        return landing.at[pl.ds(4 * b, min(4, NT - 1 - 4 * b))]

    def arrive(landing, sems, count, use):
        for b in range(4):
            @pl.when(b < count)
            def _(b=b):
                take(block(landing, b), sems.at[b])
                for a in (2 * b + 1, 2 * b + 2):
                    use(a, landing.at[2 * a - 2])
                    use(-a, landing.at[2 * a - 2 + (a < NT // 2)])

    def all_sent(landing, group, count):
        for b in range(4):
            @pl.when(b < count)
            def _(b=b):
                take(block(landing, b), send_sem.at[group])

    for dz in range(1, NZ):
        @pl.when(at_z >= dz)
        def _(dz=dz):
            meet(near_sem, (at_z - dz, t), (NZ + at_z - dz, t))

    take(halo_q.at[0], halo_sem.at[2])
    take(halo_q.at[1], halo_sem.at[3])
    for side, o, row in ((0, -1, FC - 16), (1, 1, FC + 32)):
        for b in range(2):
            for c in range(4):
                x, y = (halo_q[side, cc, 8 * b : 8 * b + 8, :] for cc in (c, 3 - c))
                fine_q[c, row + 8 * b : row + 8 * b + 8, :] = turn(x, o, True, y)

    def fill_rims(src, sem):
        for side, o, row in ((0, -1, FC - 16), (1, 1, FC + 32)):
            take(src.at[side], sem.at[side])
            for f in range(3):
                for b in range(2):
                    for c in range(4):
                        x, y = (src[side, f, cc, 8 * b : 8 * b + 8, :] for cc in (c, 3 - c))
                        fine[f, c, row + 8 * b : row + 8 * b + 8, :] = turn(x, o, f == 2, y)

    fill_rims(halo, halo_sem)
    share(rate_own, rate_ring, ring_sem.at[0], rate_blocks, 0)
    fine_run(fine, fine_e, fine_q)
    for f in range(3):
        first_end[f] = restrict(fine.at[f], FC) * 0.0625
        start = first_end[f] - restrict(own.at[f], 0) * 0.0625
        start_own[f] = start
        ring[f, CC : CC + 8, :] = start
        for c in range(4):
            first_run[f, c] = fine[f, c, FC : FC + 32, :]

    def edges():
        send(first_run.at[:, :, pl.ds(16, 16), :], halo_f.at[0], halo_sem.at[4], (k, tile_at(1)))
        send(first_run.at[:, :, pl.ds(0, 16), :], halo_f.at[1], halo_sem.at[5], (k, tile_at(-1)))

    share(start_own, start_ring, ring_sem.at[1], first_blocks, 1)
    edges()

    rates[CC : CC + 8, :] = rate_own[...]

    def use_rate(o, ref):
        rates[CC + 8 * o : CC + 8 * o + 8, :] = turn(ref[...], o, True)

    arrive(rate_ring, ring_sem.at[0], rate_blocks, use_rate)

    def use_in(whole):
        def use(o, ref):
            for f, x in enumerate(oriented(ref, o)):
                whole[f, CC + 8 * o : CC + 8 * o + 8, :] = x

        return use

    arrive(start_ring, ring_sem.at[1], first_blocks, use_in(ring))

    def chain(least, most, i):
        for m in (3, 2, 1, 0):
            def one(_, i, m=m):
                coarse(ring, ring_e, rates, CC - 12 - 16 * m, CC + 20 + 16 * m)
                for f in range(3):
                    total[f] = total[f] + ring[f, pl.ds(CC - 4, 16), :]

                @pl.when(i == j - 1)
                def _():
                    total_j[...] = total[...]

                @pl.when(i == k - 1)
                def _():
                    total_k[...] = total[...]

                return i + 1

            count = jnp.minimum(most, 4 * m + 4) - jnp.maximum(least, 4 * m)
            i = lax.fori_loop(0, jnp.maximum(count, 0), one, i)
        return i

    def fine_from(change):
        for side, o, row in ((0, -1, FC - 16), (1, 1, FC + 32)):
            for f in range(3):
                for b in range(2):
                    for c in range(4):
                        x, y = (halo_f[side, f, cc, 8 * b : 8 * b + 8, :] for cc in (c, 3 - c))
                        fine[f, c, row + 8 * b : row + 8 * b + 8, :] = turn(x, o, f == 2, y)
        for f in range(3):
            more = change[f]
            for c in range(4):
                fine[f, c, FC : FC + 32, :] = first_run[f, c]
                for p in range(4):
                    rows = pl.ds(FC - 16 + p, 16, stride=4)
                    fine[f, c, rows, :] = fine[f, c, rows, :] + more
        fine_run(fine, fine_e, fine_q)

    i = chain(n - j, n, jnp.int32(1))
    take(halo_f.at[0], halo_sem.at[4])
    take(halo_f.at[1], halo_sem.at[5])

    @pl.when(j > 0)
    def _():
        fine_from(total_j)

    for f in range(3):
        term = restrict(fine.at[f], FC) * 0.0625 - (first_end[f] + total[f, 4:12, :])
        term_own[f] = term
        work[f, CC : CC + 8, :] = term
    share(term_own, term_ring, ring_sem.at[2], last_blocks, 2)

    chain(0, n - j, i)

    @pl.when((j != k) & (k > 0))
    def _():
        fine_from(total_k)

    @pl.when(k == 0)
    def _():
        for f in range(3):
            for c in range(4):
                fine[f, c, FC : FC + 32, :] = first_run[f, c]


    apart_out = lane // 4
    phase = lax.rem(lane, 4)
    for f in range(3):
        for b in range(4):
            x = [fine[f, c, FC + 8 * b : FC + 8 * b + 8, :] for c in range(4)]
            for s in range(4):
                y = [gather(x[c], apart_out + 32 * s) for c in range(4)]
                fine_out[f, 8 * b : 8 * b + 8, 128 * s : 128 * s + 128] = jnp.where(
                    phase < 2, jnp.where(phase == 0, y[0], y[1]), jnp.where(phase == 2, y[2], y[3])
                )

    keep = pltpu.make_async_copy(fine_out, out, load_sem.at[0])
    keep.start()
    arrive(term_ring, ring_sem.at[2], last_blocks, use_in(work))

    @pl.when(at_z < NZ - 1)
    def _():
        pl.semaphore_wait(near_sem, 2 * (NZ - 1 - at_z))


    last = jnp.where(j == 0, 0, NK - 1 - j)
    m = jnp.int32(0)
    for group in (3, 2, 1, 0):
        def power(s, m, group=group):
            coarse(work, ring_e, rates, CC - 12 - 16 * group, CC + 20 + 16 * group)
            powers[m] = work[:, CC : CC + 8, :]

            @pl.when(j + m + 1 != k)
            def _():
                send(powers.at[m], power_in.at[m], power_sem.at[m], (j + m + 1, t), 3)

            @pl.when(j + m + 1 == k)
            def _():
                pltpu.make_async_copy(powers.at[m], power_in.at[m], power_sem.at[m]).start()

            return m + 1

        m = lax.fori_loop(0, jnp.clip(last - 4 * group, 0, 4), power, m)

    all_sent(term_ring, 2, last_blocks)
    term_own[...] = jnp.zeros((3, 8, 128), jnp.float32)

    def add(m, carry):
        take(power_in.at[m], power_sem.at[m])
        term_own[...] = term_own[...] + power_in[m]
        return carry

    lax.fori_loop(0, k - 1, add, 0)

    change[...] = term_own[...]
    keep.wait()

    for _ in range(2):
        take(halo, send_sem.at[0])
    take(halo_q, send_sem.at[0])
    all_sent(rate_ring, 0, rate_blocks)
    all_sent(start_ring, 1, first_blocks)

    def sent(m, carry):
        take(powers.at[m], send_sem.at[3])
        return carry

    lax.fori_loop(0, last - jnp.where((j > 0) & (k > j), 1, 0), sent, 0)


def finish(fine, change, out, fine_in, change_in, sems):
    loads = [pltpu.make_async_copy(fine.at[f], fine_in.at[f], sems.at[f]) for f in range(3)]
    stores = [pltpu.make_async_copy(fine_in.at[f], out.at[0, f], sems.at[f]) for f in range(3)]
    load_change = pltpu.make_async_copy(change, change_in, sems.at[3])
    load_change.start()
    for load in loads:
        load.start()
    load_change.wait()
    wide = lax.broadcasted_iota(jnp.int32, (8, 128), 1) // 4
    first = lax.broadcasted_iota(jnp.int32, (8, 128), 0) < 4
    for f in range(3):
        more = [gather(change_in[f], wide + 32 * s) for s in range(4)]
        loads[f].wait()
        for s in range(4):
            for b in range(4):
                upper, lower = (jnp.broadcast_to(more[s][r : r + 1, :], (8, 128)) for r in (2 * b, 2 * b + 1))
                at = (f, slice(8 * b, 8 * b + 8), slice(128 * s, 128 * s + 128))
                fine_in[at] = fine_in[at] + jnp.where(first, upper, lower)
        stores[f].start()
    for store in stores:
        store.wait()


def body(initial, rotation, seam_flip):
    def vmem(*shape):
        return pltpu.VMEM(shape, jnp.float32)

    dma = pltpu.SemaphoreType.DMA
    scratch = [
        vmem(3, 32, 512), vmem(32, 512),
        vmem(3, 4, 32, 128), vmem(4, 32, 128),
        vmem(2, 3, 4, 16, 128), vmem(2, 4, 16, 128),
        vmem(3, 4, FR, 128), vmem(4, FR, 128), vmem(4, FR, 128),
        vmem(3, 4, 32, 128), vmem(2, 3, 4, 16, 128),
        vmem(CR, 128), vmem(8, 128), vmem(NT - 1, 8, 128),
        vmem(3, 8, 128), vmem(NT - 1, 3, 8, 128),
        vmem(3, CR, 128), vmem(CR, 128),
        vmem(3, 16, 128), vmem(3, 16, 128), vmem(3, 16, 128), vmem(3, 8, 128),
        vmem(3, CR, 128),
        vmem(3, 8, 128), vmem(NT - 1, 3, 8, 128),
        vmem(NK - 1, 3, 8, 128), vmem(NK - 1, 3, 8, 128),
        vmem(3, 32, 512),
        dma((2,)), dma((4,)), dma((6,)), dma((3, 4)), dma((NK - 1,)), pltpu.SemaphoreType.REGULAR,
    ]
    fine, change = pl.pallas_call(
        kernel,
        out_shape=(
            jax.ShapeDtypeStruct((3, 32, 512), jnp.float32),
            jax.ShapeDtypeStruct((3, 8, 128), jnp.float32),
        ),
        in_specs=[
            pl.BlockSpec(memory_space=pl.ANY),
            pl.BlockSpec(memory_space=pl.ANY),
            pl.BlockSpec(memory_space=pltpu.SMEM),
        ],
        out_specs=(pl.BlockSpec(memory_space=pl.ANY), pl.BlockSpec(memory_space=pltpu.VMEM)),
        scratch_shapes=scratch,
        compiler_params=pltpu.CompilerParams(
            collective_id=0, has_side_effects=True, vmem_limit_bytes=60 * 1024 * 1024
        ),
        name="parareal",
    )(initial, rotation, seam_flip)
    return pl.pallas_call(
        finish,
        out_shape=jax.ShapeDtypeStruct((1, 3, 32, 512), jnp.float32),
        in_specs=[pl.BlockSpec(memory_space=pl.ANY)] * 2,
        out_specs=pl.BlockSpec(memory_space=pl.ANY),
        scratch_shapes=[vmem(3, 32, 512), vmem(3, 8, 128), dma((4,))],
        compiler_params=pltpu.CompilerParams(vmem_limit_bytes=60 * 1024 * 1024),
        name="finish",
    )(fine, change)


def solution(mesh):
    in_specs = (P(None, "tile", None), P("tile", None), P())
    out_specs = P("tm", None, "tile", None)
    return jax.shard_map(body, mesh=mesh, in_specs=in_specs, out_specs=out_specs, check_vma=False)
```

```python
import jax
import jax.numpy as jnp
from jax import lax
from jax.experimental import pallas as pl
from jax.experimental.pallas import tpu as pltpu
from jax.sharding import PartitionSpec as P

MESH = pl.DeviceIdType.MESH
NT = 16
NK = 16
HC = 0.45
FC = 24
FR = 88
CC = 80
CR = 168
NZ = 8
OTHERS = tuple((x, y, c) for y in (2, 1, 3, 0) for x in (1, 0) for c in (1, 0) if (x, y, c) != (0, 0, 0))


def gather(x, idx):
    return jnp.take_along_axis(x, idx, axis=1)


def ahead(x):
    return pltpu.roll(x, 127, 1)


def behind(x):
    return pltpu.roll(x, 1, 1)


def blocks(first, past):
    return range(first // 8 * 8, -(-past // 8) * 8, 8)


def coarse_step(st, e_ref, q, first, past):
    for r in blocks(first - 1, past + 1):
        g = st[0, r : r + 8, :] - HC * (st[1, r + 1 : r + 9, :] - st[1, r - 1 : r + 7, :])
        v = st[2, r : r + 8, :]
        wide = pltpu.roll(v, 126, 1) - 2.0 * v + pltpu.roll(v, 2, 1)
        st[0, r : r + 8, :] = g - HC * (ahead(v) - behind(v))
        e_ref[r : r + 8, :] = HC * ((ahead(g) - behind(g)) - HC * wide)
    for r in blocks(first, past):
        u, v, rate = st[1, r : r + 8, :], st[2, r : r + 8, :], q[r : r + 8, :]
        new = u + rate * v - HC * (st[0, r + 1 : r + 9, :] - st[0, r - 1 : r + 7, :])
        st[1, r : r + 8, :] = new
        st[2, r : r + 8, :] = v - rate * new - e_ref[r : r + 8, :]


def coarse(st, e_ref, q, first, past):
    coarse_step(st, e_ref, q, first - 2, past + 2)
    coarse_step(st, e_ref, q, first, past)


def fine_step(st, e_ref, q, first, past):
    for r in blocks(first - 1, past + 1):
        v = [st[2, c, r : r + 8, :] for c in range(4)]
        g = [st[0, c, r : r + 8, :] - HC * (st[1, c, r + 1 : r + 9, :] - st[1, c, r - 1 : r + 7, :]) for c in range(4)]
        vs = [behind(v[2]), behind(v[3])] + v + [ahead(v[0]), ahead(v[1])]
        gs = [behind(g[3])] + g + [ahead(g[0])]
        for c in range(4):
            st[0, c, r : r + 8, :] = g[c] - HC * (vs[c + 3] - vs[c + 1])
            e_ref[c, r : r + 8, :] = HC * ((gs[c + 2] - gs[c]) - HC * (vs[c + 4] - 2.0 * v[c] + vs[c]))
    for r in blocks(first, past):
        for c in range(4):
            u, v, rate = st[1, c, r : r + 8, :], st[2, c, r : r + 8, :], q[c, r : r + 8, :]
            new = u + rate * v - HC * (st[0, c, r + 1 : r + 9, :] - st[0, c, r - 1 : r + 7, :])
            st[1, c, r : r + 8, :] = new
            st[2, c, r : r + 8, :] = v - rate * new - e_ref[c, r : r + 8, :]


def fine_run(st, e_ref, q):
    for s in range(8):
        fine_step(st, e_ref, q, FC - 14 + 2 * s, FC + 46 - 2 * s)


def restrict(ref, first):
    total = None
    for j in range(4):
        for c in range(4):
            part = ref[c, pl.ds(first + j, 8, stride=4), :]
            total = part if total is None else total + part
    return total


def kernel(initial, rotation, flips, out, change, xin, rin, own, own_q, halo, halo_q, fine, fine_q, fine_e, first_run, halo_f,
           rates, rate_own, rate_ring, start_own, start_ring, ring, ring_e, total, total_j, total_k, first_end, work, term_own, term_ring,
           powers, power_in, fine_out, load_sem, send_sem, halo_sem, ring_sem, power_sem, near_sem):
    k = lax.axis_index("tm")
    t = lax.axis_index("tile")
    lane = lax.broadcasted_iota(jnp.int32, (8, 128), 1)
    turned = 127 - lane

    def tile_at(o):
        return lax.rem(t + (o + NT), NT)

    load_x = pltpu.make_async_copy(initial, xin, load_sem.at[0])
    load_q = pltpu.make_async_copy(rotation, rin, load_sem.at[1])
    load_x.start()
    load_q.start()

    at_xh, at_z = k // NZ, lax.rem(k, NZ)
    at_xl, at_y, at_core = t // 8, lax.rem(t // 2, 4), lax.rem(t, 2)

    def place(dx=0, dy=0, dz=0, dc=0):
        px = lax.rem(2 * at_xh + at_xl + (dx + 4), 4)
        return (
            (px // 2) * NZ + lax.rem(at_z + (dz + NZ), NZ),
            lax.rem(px, 2) * 8 + lax.rem(at_y + (dy + 4), 4) * 2 + lax.rem(at_core + dc, 2),
        )

    def meet(sem, *where):
        for there in where:
            pl.semaphore_signal(sem, inc=1, device_id=there, device_id_type=MESH)

    barrier = pltpu.get_barrier_semaphore()
    meet(barrier, *((k, tile_at(o)) for o in (1, -1, 8, 4, -4, 2, -2, 3, -3, 5, -5, 6, -6, 7, -7)), place(dx=2))
    for dz in range(1, NZ):
        @pl.when(at_z + dz < NZ)
        def _(dz=dz):
            meet(barrier, (at_z + dz, t), (NZ + at_z + dz, t))

    j = jnp.where(k < 4, jnp.where(k == 0, 8, k), jnp.where(k < 8, k + 8, jnp.where(k < 12, k - 4, k - 3)))
    j = jnp.where(k == 7, 0, jnp.where(k == 15, 15, j))
    n = jnp.maximum(j, k)

    odd = {0: None}
    up = down = jnp.int32(0)
    for o in range(1, NT // 2 + 1):
        up = up + jnp.where(flips[tile_at(o)] != 0, 1, 0)
        down = down + jnp.where(flips[tile_at(1 - o)] != 0, 1, 0)
        odd[o] = (jnp.zeros((8, 128), jnp.int32) + lax.rem(up, 2)) != 0
        odd[-o] = (jnp.zeros((8, 128), jnp.int32) + lax.rem(down, 2)) != 0

    def turn(x, o, negate, other=None):
        if o == 0:
            return x
        back = gather(x if other is None else other, turned)
        return jnp.where(odd[o], -back if negate else back, x)

    def oriented(src, o):
        return [turn(src[f], o, f == 2) for f in range(3)]

    zero = jnp.zeros((8, 128), jnp.float32)
    for f in range(3):
        for b in range(CR // 8):
            work[f, 8 * b : 8 * b + 8, :] = zero
        for b in (0, 1, CR // 8 - 2, CR // 8 - 1):
            ring[f, 8 * b : 8 * b + 8, :] = zero
        for c in range(4):
            for b in (0, FR // 8 - 2, FR // 8 - 1):
                fine[f, c, 8 * b : 8 * b + 8, :] = zero
        for ref in (total, total_j, total_k):
            ref[f] = jnp.zeros((16, 128), jnp.float32)
    for b in (0, 1, CR // 8 - 2, CR // 8 - 1):
        rates[8 * b : 8 * b + 8, :] = zero
    for c in range(4):
        for b in (0, FR // 8 - 2, FR // 8 - 1):
            fine_q[c, 8 * b : 8 * b + 8, :] = zero

    quarter = lane // 32
    apart = 4 * lax.rem(lane, 32)

    def spread(load, store):
        x = [load(s) for s in range(4)]
        for c in range(4):
            y = [gather(x[s], apart + c) for s in range(4)]
            store(c, jnp.where(quarter < 2, jnp.where(quarter == 0, y[0], y[1]), jnp.where(quarter == 2, y[2], y[3])))

    load_q.wait()
    for b in range(4):
        def store_q(c, x, b=b):
            own_q[c, 8 * b : 8 * b + 8, :] = x
            fine_q[c, FC + 8 * b : FC + 8 * b + 8, :] = x

        spread(lambda s, b=b: rin[8 * b : 8 * b + 8, 128 * s : 128 * s + 128], store_q)
    load_x.wait()
    for f in range(3):
        for b in range(4):
            def store_x(c, x, f=f, b=b):
                own[f, c, 8 * b : 8 * b + 8, :] = x
                fine[f, c, FC + 8 * b : FC + 8 * b + 8, :] = x

            spread(lambda s, f=f, b=b: xin[f, 8 * b : 8 * b + 8, 128 * s : 128 * s + 128], store_x)

    pl.semaphore_wait(barrier, NT + 2 * at_z)

    def send(src, dst, recv, where, group=0):
        pltpu.make_async_remote_copy(
            src_ref=src, dst_ref=dst, send_sem=send_sem.at[group], recv_sem=recv, device_id=where, device_id_type=MESH
        ).start()

    def take(ref, sem):
        pltpu.make_async_copy(ref, ref, sem).wait()

    send(own.at[:, :, pl.ds(16, 16), :], halo.at[0], halo_sem.at[0], (k, tile_at(1)))
    send(own.at[:, :, pl.ds(0, 16), :], halo.at[1], halo_sem.at[1], (k, tile_at(-1)))
    send(own_q.at[:, pl.ds(16, 16), :], halo_q.at[0], halo_sem.at[2], (k, tile_at(1)))
    send(own_q.at[:, pl.ds(0, 16), :], halo_q.at[1], halo_sem.at[3], (k, tile_at(-1)))
    rate_own[...] = restrict(own_q, 0) * 0.25

    first_blocks = (n + 3) // 4
    last_blocks = jnp.where(j == 0, 0, (NK + 2 - j) // 4)
    rate_blocks = jnp.maximum(first_blocks, last_blocks)

    def share(src, landing, sems, count, group):
        for dx, dy, dc in OTHERS:
            there = lax.rem(at_xl + dx, 2) * 8 + lax.rem(at_y + dy, 4) * 2 + lax.rem(at_core + dc, 2)
            delta = lax.rem(there - t + NT, NT)
            far = jnp.minimum(delta, NT - delta)
            slot = 2 * (far - 1) + jnp.where(delta < 8, 1, 0)

            @pl.when((far - 1) // 2 < count)
            def _(there=there, far=far, slot=slot):
                send(src, landing.at[slot], sems.at[(far - 1) // 2], (k, there), group)

    def block(landing, b):
        return landing.at[pl.ds(4 * b, min(4, NT - 1 - 4 * b))]

    def arrive(landing, sems, count, use):
        for b in range(4):
            @pl.when(b < count)
            def _(b=b):
                take(block(landing, b), sems.at[b])
                for a in (2 * b + 1, 2 * b + 2):
                    use(a, landing.at[2 * a - 2])
                    use(-a, landing.at[2 * a - 2 + (a < NT // 2)])

    def all_sent(landing, group, count):
        for b in range(4):
            @pl.when(b < count)
            def _(b=b):
                take(block(landing, b), send_sem.at[group])

    for dz in range(1, NZ):
        @pl.when(at_z >= dz)
        def _(dz=dz):
            meet(near_sem, (at_z - dz, t), (NZ + at_z - dz, t))

    take(halo_q.at[0], halo_sem.at[2])
    take(halo_q.at[1], halo_sem.at[3])
    for side, o, row in ((0, -1, FC - 16), (1, 1, FC + 32)):
        for b in range(2):
            for c in range(4):
                x, y = (halo_q[side, cc, 8 * b : 8 * b + 8, :] for cc in (c, 3 - c))
                fine_q[c, row + 8 * b : row + 8 * b + 8, :] = turn(x, o, True, y)

    def fill_rims(src, sem):
        for side, o, row in ((0, -1, FC - 16), (1, 1, FC + 32)):
            take(src.at[side], sem.at[side])
            for f in range(3):
                for b in range(2):
                    for c in range(4):
                        x, y = (src[side, f, cc, 8 * b : 8 * b + 8, :] for cc in (c, 3 - c))
                        fine[f, c, row + 8 * b : row + 8 * b + 8, :] = turn(x, o, f == 2, y)

    fill_rims(halo, halo_sem)
    share(rate_own, rate_ring, ring_sem.at[0], rate_blocks, 0)
    fine_run(fine, fine_e, fine_q)
    for f in range(3):
        first_end[f] = restrict(fine.at[f], FC) * 0.0625
        start = first_end[f] - restrict(own.at[f], 0) * 0.0625
        start_own[f] = start
        ring[f, CC : CC + 8, :] = start
        for c in range(4):
            first_run[f, c] = fine[f, c, FC : FC + 32, :]

    def edges():
        send(first_run.at[:, :, pl.ds(16, 16), :], halo_f.at[0], halo_sem.at[4], (k, tile_at(1)))
        send(first_run.at[:, :, pl.ds(0, 16), :], halo_f.at[1], halo_sem.at[5], (k, tile_at(-1)))

    share(start_own, start_ring, ring_sem.at[1], first_blocks, 1)
    edges()

    rates[CC : CC + 8, :] = rate_own[...]

    def use_rate(o, ref):
        rates[CC + 8 * o : CC + 8 * o + 8, :] = turn(ref[...], o, True)

    arrive(rate_ring, ring_sem.at[0], rate_blocks, use_rate)

    def use_in(whole):
        def use(o, ref):
            for f, x in enumerate(oriented(ref, o)):
                whole[f, CC + 8 * o : CC + 8 * o + 8, :] = x

        return use

    arrive(start_ring, ring_sem.at[1], first_blocks, use_in(ring))

    def chain(least, most, i):
        for m in (3, 2, 1, 0):
            def one(_, i, m=m):
                coarse(ring, ring_e, rates, CC - 12 - 16 * m, CC + 20 + 16 * m)
                for f in range(3):
                    total[f] = total[f] + ring[f, pl.ds(CC - 4, 16), :]

                @pl.when(i == j - 1)
                def _():
                    total_j[...] = total[...]

                @pl.when(i == k - 1)
                def _():
                    total_k[...] = total[...]

                return i + 1

            count = jnp.minimum(most, 4 * m + 4) - jnp.maximum(least, 4 * m)
            i = lax.fori_loop(0, jnp.maximum(count, 0), one, i)
        return i

    def fine_from(change):
        for side, o, row in ((0, -1, FC - 16), (1, 1, FC + 32)):
            for f in range(3):
                for b in range(2):
                    for c in range(4):
                        x, y = (halo_f[side, f, cc, 8 * b : 8 * b + 8, :] for cc in (c, 3 - c))
                        fine[f, c, row + 8 * b : row + 8 * b + 8, :] = turn(x, o, f == 2, y)
        for f in range(3):
            more = change[f]
            for c in range(4):
                fine[f, c, FC : FC + 32, :] = first_run[f, c]
                for p in range(4):
                    rows = pl.ds(FC - 16 + p, 16, stride=4)
                    fine[f, c, rows, :] = fine[f, c, rows, :] + more
        fine_run(fine, fine_e, fine_q)

    i = chain(n - j, n, jnp.int32(1))
    take(halo_f.at[0], halo_sem.at[4])
    take(halo_f.at[1], halo_sem.at[5])

    @pl.when(j > 0)
    def _():
        fine_from(total_j)

    for f in range(3):
        term = restrict(fine.at[f], FC) * 0.0625 - (first_end[f] + total[f, 4:12, :])
        term_own[f] = term
        work[f, CC : CC + 8, :] = term
    share(term_own, term_ring, ring_sem.at[2], last_blocks, 2)

    chain(0, n - j, i)

    @pl.when((j != k) & (k > 0))
    def _():
        fine_from(total_k)

    @pl.when(k == 0)
    def _():
        for f in range(3):
            for c in range(4):
                fine[f, c, FC : FC + 32, :] = first_run[f, c]


    apart_out = lane // 4
    phase = lax.rem(lane, 4)
    for f in range(3):
        for b in range(4):
            x = [fine[f, c, FC + 8 * b : FC + 8 * b + 8, :] for c in range(4)]
            for s in range(4):
                y = [gather(x[c], apart_out + 32 * s) for c in range(4)]
                fine_out[f, 8 * b : 8 * b + 8, 128 * s : 128 * s + 128] = jnp.where(
                    phase < 2, jnp.where(phase == 0, y[0], y[1]), jnp.where(phase == 2, y[2], y[3])
                )

    keep = pltpu.make_async_copy(fine_out, out, load_sem.at[0])
    keep.start()
    arrive(term_ring, ring_sem.at[2], last_blocks, use_in(work))

    @pl.when(at_z < NZ - 1)
    def _():
        pl.semaphore_wait(near_sem, 2 * (NZ - 1 - at_z))


    last = jnp.where(j == 0, 0, NK - 1 - j)
    m = jnp.int32(0)
    for group in (3, 2, 1, 0):
        def power(s, m, group=group):
            coarse(work, ring_e, rates, CC - 12 - 16 * group, CC + 20 + 16 * group)
            powers[m] = work[:, CC : CC + 8, :]

            @pl.when(j + m + 1 != k)
            def _():
                send(powers.at[m], power_in.at[m], power_sem.at[m], (j + m + 1, t), 3)

            @pl.when(j + m + 1 == k)
            def _():
                pltpu.make_async_copy(powers.at[m], power_in.at[m], power_sem.at[m]).start()

            return m + 1

        m = lax.fori_loop(0, jnp.clip(last - 4 * group, 0, 4), power, m)

    all_sent(term_ring, 2, last_blocks)
    term_own[...] = jnp.zeros((3, 8, 128), jnp.float32)

    def add(m, carry):
        take(power_in.at[m], power_sem.at[m])
        term_own[...] = term_own[...] + power_in[m]
        return carry

    lax.fori_loop(0, k - 1, add, 0)

    change[...] = term_own[...]
    keep.wait()

    for _ in range(2):
        take(halo, send_sem.at[0])
    take(halo_q, send_sem.at[0])
    all_sent(rate_ring, 0, rate_blocks)
    all_sent(start_ring, 1, first_blocks)

    def sent(m, carry):
        take(powers.at[m], send_sem.at[3])
        return carry

    lax.fori_loop(0, last - jnp.where((j > 0) & (k > j), 1, 0), sent, 0)


def finish(fine, change, out, fine_in, change_in, sems):
    loads = [pltpu.make_async_copy(fine.at[f], fine_in.at[f], sems.at[f]) for f in range(3)]
    stores = [pltpu.make_async_copy(fine_in.at[f], out.at[0, f], sems.at[f]) for f in range(3)]
    load_change = pltpu.make_async_copy(change, change_in, sems.at[3])
    load_change.start()
    for load in loads:
        load.start()
    load_change.wait()
    wide = lax.broadcasted_iota(jnp.int32, (8, 128), 1) // 4
    first = lax.broadcasted_iota(jnp.int32, (8, 128), 0) < 4
    for f in range(3):
        more = [gather(change_in[f], wide + 32 * s) for s in range(4)]
        loads[f].wait()
        for s in range(4):
            for b in range(4):
                upper, lower = (jnp.broadcast_to(more[s][r : r + 1, :], (8, 128)) for r in (2 * b, 2 * b + 1))
                at = (f, slice(8 * b, 8 * b + 8), slice(128 * s, 128 * s + 128))
                fine_in[at] = fine_in[at] + jnp.where(first, upper, lower)
        stores[f].start()
    for store in stores:
        store.wait()


def body(initial, rotation, seam_flip):
    def vmem(*shape):
        return pltpu.VMEM(shape, jnp.float32)

    dma = pltpu.SemaphoreType.DMA
    scratch = [
        vmem(3, 32, 512), vmem(32, 512),
        vmem(3, 4, 40, 128), vmem(4, 40, 128),
        vmem(2, 3, 4, 16, 128), vmem(2, 4, 16, 128),
        vmem(3, 4, FR, 128), vmem(4, FR, 128), vmem(4, FR, 128),
        vmem(3, 4, 32, 128), vmem(2, 3, 4, 16, 128),
        vmem(CR, 128), vmem(8, 128), vmem(NT - 1, 8, 128),
        vmem(3, 8, 128), vmem(NT - 1, 3, 8, 128),
        vmem(3, CR, 128), vmem(CR, 128),
        vmem(3, 16, 128), vmem(3, 16, 128), vmem(3, 16, 128), vmem(3, 8, 128),
        vmem(3, CR, 128),
        vmem(3, 8, 128), vmem(NT - 1, 3, 8, 128),
        vmem(NK - 1, 3, 8, 128), vmem(NK - 1, 3, 8, 128),
        vmem(3, 32, 512),
        dma((2,)), dma((4,)), dma((6,)), dma((3, 4)), dma((NK - 1,)), pltpu.SemaphoreType.REGULAR,
    ]
    fine, change = pl.pallas_call(
        kernel,
        out_shape=(
            jax.ShapeDtypeStruct((3, 32, 512), jnp.float32),
            jax.ShapeDtypeStruct((3, 8, 128), jnp.float32),
        ),
        in_specs=[
            pl.BlockSpec(memory_space=pl.ANY),
            pl.BlockSpec(memory_space=pl.ANY),
            pl.BlockSpec(memory_space=pltpu.SMEM),
        ],
        out_specs=(pl.BlockSpec(memory_space=pl.ANY), pl.BlockSpec(memory_space=pltpu.VMEM)),
        scratch_shapes=scratch,
        compiler_params=pltpu.CompilerParams(
            collective_id=0, has_side_effects=True, vmem_limit_bytes=60 * 1024 * 1024
        ),
        name="parareal",
    )(initial, rotation, seam_flip)
    return pl.pallas_call(
        finish,
        out_shape=jax.ShapeDtypeStruct((1, 3, 32, 512), jnp.float32),
        in_specs=[pl.BlockSpec(memory_space=pl.ANY)] * 2,
        out_specs=pl.BlockSpec(memory_space=pl.ANY),
        scratch_shapes=[vmem(3, 32, 512), vmem(3, 8, 128), dma((4,))],
        compiler_params=pltpu.CompilerParams(vmem_limit_bytes=60 * 1024 * 1024),
        name="finish",
    )(fine, change)


def solution(mesh):
    in_specs = (P(None, "tile", None), P("tile", None), P())
    out_specs = P("tm", None, "tile", None)
    return jax.shard_map(body, mesh=mesh, in_specs=in_specs, out_specs=out_specs, check_vma=False)
```
